512 devices in a mesh: dom: 32 (over y, x), grp: 16 (over z, core).
Axes of the slice: x: 4, y: 8, z: 8, core: 2. Of those that a mesh axis runs over, the one named last changes fastest.
Arguments:
- features: float32 [262144, 128], P(('dom', 'grp')), may hold values from -6 to 6
- w_self: float32 [128, 128], replicated, may hold values from -0.5 to 0.5
- w_neigh: float32 [128, 128], replicated, may hold values from -0.5 to 0.5
- bias: float32 [128], replicated, may hold values from -3 to 3
- cotangent: float32 [262144, 128], P(('dom', 'grp')), may hold values from -6 to 6
- neighbours: int32 [10, 262144], P(None, ('dom', 'grp')), may hold values from 0 to 1279
- degree: int32 [262144], P(('dom', 'grp')), may hold values from 1 to 10
- halo_rows: int32 [65536], P(('dom', 'grp')), may hold values from 0 to 511
- send_rows: int32 [32, 16, 32, 16], P('dom', 'grp'), may hold values from 0 to 511
Outputs:
- activated: float32 [262144, 128], P(('dom', 'grp'))
- grad_features: float32 [262144, 128], P(('dom', 'grp'))
- grad_w_self: float32 [128, 128], replicated
- grad_w_neigh: float32 [128, 128], replicated
- grad_bias: float32 [128], replicated
The draws below stay inside these ranges and needn't reach their ends.
Inputs may be any that keep to these rules, and one draw needn't show every extreme that they name: `neighbours`: A row of the source table of the vertex's own device; slots s >= degree hold a row too and are ignored. `halo_rows`: local row numbers; a row may be listed more than once. `send_rows`: local row numbers of the sending device; a row may be listed more than once.
All inputs are finite; a program needn't handle non-finite values.
Results may differ from the reference program's by a relative error of at most 0.00008.
Values sent between devices are 32-bit elements; how exact they have to be, the bound alone decides.
A program may use at most 64 MiB of HBM per device.

```python
import jax
import jax.numpy as jnp
from jax import lax

FEAT = 128
HIDDEN_SIZE = 128
NODE_DEV = 512
FANOUT = 10
HALO = 128
SEND = 16
SRC = 1280
NODES = 262144
HALO_ALL = 65536
N_DOM = 32
N_GRP = 16


def set_ends(values, rng, smallest, high):
    dims = values.shape
    index_at = [jax.random.randint(jax.random.fold_in(rng, axis), (), 0, dims[axis]) for axis in range(len(dims))]
    values = values.at[tuple(index_at)].set(smallest)
    longest = dims.index(max(dims))
    index_at[longest] = (index_at[longest] + 1) % dims[longest]
    return values.at[tuple(index_at)].set(high)


def levels(key, dims, split, low, top_value):
    factor_of, own = 1.0, jax.random.fold_in(key, 6)
    for dim, shards_of in split:
        heights = jnp.exp(jax.random.uniform(jax.random.fold_in(own, dim), (shards_of,), jnp.float32, low / len(split), top_value / len(split)))
        factor_of = factor_of * jnp.repeat(heights, dims[dim] // shards_of).reshape([-1 if axis == dim else 1 for axis in range(len(dims))])
    return factor_of


def centred(rng, dims, scale, bound, split=(), kind=jnp.bfloat16):
    values = jax.random.normal(rng, dims, jnp.float32) * scale
    if len(split) > 0:
        values = levels(rng, dims, split, -0.22, 0.18) * values
    return jnp.clip(values, min=-bound, max=bound).astype(kind)


def setup_inputs(seed: int = 0) -> dict:
    seeds = jax.random.split(jax.random.key(seed), 10)
    return {
        "features": centred(seeds[0], (NODES, FEAT), 1.0, 6.0, ((0, 512),), jnp.float32),
        "w_self": centred(seeds[1], (FEAT, HIDDEN_SIZE), FEAT ** -0.5, 0.5, (), jnp.float32),
        "w_neigh": centred(seeds[2], (FEAT, HIDDEN_SIZE), FEAT ** -0.5, 0.5, (), jnp.float32),
        "bias": centred(seeds[3], (HIDDEN_SIZE,), 0.5, 3.0, (), jnp.float32),
        "cotangent": centred(seeds[4], (NODES, HIDDEN_SIZE), 1.0, 6.0, ((0, 512),), jnp.float32),
        "neighbours": set_ends(jax.random.randint(seeds[5], (FANOUT, NODES), 0, SRC), jax.random.fold_in(seeds[5], 1), 0, SRC - 1).astype(jnp.int32),
        "degree": set_ends(jax.random.randint(seeds[6], (NODES,), 1, FANOUT + 1), jax.random.fold_in(seeds[6], 1), 1, FANOUT).astype(jnp.int32),
        "halo_rows": set_ends(jax.random.randint(seeds[7], (HALO_ALL,), 0, NODE_DEV), jax.random.fold_in(seeds[7], 1), 0, NODE_DEV - 1).astype(jnp.int32),
        "send_rows": set_ends(jax.random.randint(seeds[8], (N_DOM, N_GRP, N_DOM, SEND), 0, NODE_DEV), jax.random.fold_in(seeds[8], 1), 0, NODE_DEV - 1).astype(jnp.int32),
    }


def source_map(halo_rows, send_rows):
    device_ids = jnp.arange(N_DOM * N_GRP, dtype=jnp.int32).reshape(N_DOM, N_GRP)
    row_base = device_ids * NODE_DEV
    local_rows = row_base[:, :, None] + jnp.arange(NODE_DEV, dtype=jnp.int32)[None, None, :]
    shared = row_base[:, :, None] + halo_rows.reshape(N_DOM, N_GRP, HALO).astype(jnp.int32)
    from_lower = jnp.roll(shared, 1, axis=1)
    from_upper = jnp.roll(shared, -1, axis=1)
    boundary = row_base[:, :, None, None] + send_rows.astype(jnp.int32)
    received = jnp.transpose(boundary, (2, 1, 0, 3)).reshape(N_DOM, N_GRP, N_DOM * SEND)
    table = jnp.concatenate([local_rows, from_lower, from_upper, received], axis=2)
    return table.reshape(N_DOM * N_GRP, SRC)

def reference(features, w_self, w_neigh, bias, cotangent, neighbours, degree, halo_rows, send_rows):
    highest = lax.Precision.HIGHEST
    table = source_map(halo_rows, send_rows)
    slots = neighbours.reshape(FANOUT, N_DOM * N_GRP, NODE_DEV).astype(jnp.int32)
    device_ids = jnp.arange(N_DOM * N_GRP, dtype=jnp.int32)[None, :, None]
    global_rows = table[device_ids, slots].reshape(FANOUT, NODES)
    live_mask = (jnp.arange(FANOUT, dtype=jnp.int32)[:, None] < degree[None, :]).astype(jnp.float32)
    inverse_degree = 1.0 / degree.astype(jnp.float32)

    def forward(feats, weight_self, weight_neigh, offset):
        total = jnp.zeros((NODES, FEAT), jnp.float32)
        for step in range(FANOUT):
            total = total + feats[global_rows[step]] * live_mask[step][:, None]
        aggregate = total * inverse_degree[:, None]
        pre = jnp.dot(feats, weight_self, precision=highest, preferred_element_type=jnp.float32)
        pre = pre + jnp.dot(aggregate, weight_neigh, precision=highest, preferred_element_type=jnp.float32)
        return jax.nn.gelu(pre + offset, approximate=True)
    activated, pullback = jax.vjp(forward, features, w_self, w_neigh, bias)
    grad_x, grad_ws, grad_wn, grad_b = pullback(cotangent)
    scale = 1.0 / jnp.sqrt(jnp.float32(NODES))
    return (activated, grad_x, grad_ws * scale, grad_wn * scale, grad_b * scale)
```

```python
import functools

import jax
import jax.numpy as jnp
from jax import lax
from jax.experimental import pallas as pl
from jax.experimental.pallas import tpu as pltpu
from jax.sharding import PartitionSpec as P

MESH = pl.DeviceIdType.MESH
F32 = jnp.float32
BF16 = jnp.bfloat16


def halves(value):
    high = value.astype(BF16)
    low = (value - high.astype(F32)).astype(BF16)
    return high, low


def stacked(value):
    return jnp.concatenate(halves(value), axis=0)


def beside(value):
    return jnp.concatenate(halves(value), axis=1)


def folded_rows(product):
    count = product.shape[0] // 2
    return product[:count] + product[count:]


def folded_columns(product):
    count = product.shape[1] // 2
    return product[:, :count] + product[:, count:]


def weight_pair(weight):
    high, low = halves(weight)
    return jnp.concatenate(
        [jnp.concatenate([high, high], axis=1), jnp.concatenate([low, low], axis=1)], axis=0
    )


def matmul(left, right):
    return jnp.dot(left, right, preferred_element_type=F32)


def matmul_nt(left, right):
    return lax.dot_general(left, right, (((1,), (1,)), ((), ())), preferred_element_type=F32)


def kernel(
    partitions,
    groups,
    width_x,
    scale,
    features_hbm,
    w_self_hbm,
    w_neigh_hbm,
    bias_hbm,
    cotangent_hbm,
    neighbours_hbm,
    degree_hbm,
    halo_hbm,
    send_hbm,
    activated_hbm,
    grad_features_hbm,
    grad_ws_hbm,
    grad_wn_hbm,
    grad_b_hbm,
    features,
    w_self,
    w_neigh,
    bias,
    cotangent,
    neighbours,
    degree,
    halo,
    send,
    counts,
    placement,
    outgoing,
    table,
    table_grad,
    back,
    activated,
    grad_features,
    weight_grad,
    bias_grad,
    scatter_slots,
    bias_slots,
    x_slots,
    y_slots,
    piece,
    gathered,
    total_b,
    in_sem,
    out_sem,
    send_sem,
    recv_sem,
):
    node_count, feat = features.shape
    halo_count = halo.shape[1]
    send_count = send.shape[1]
    slot_count = neighbours.shape[0]
    remote_rows = table.shape[0]
    table_rows = node_count + remote_rows
    width_y = partitions // width_x
    piece_rows = 2 * feat // groups

    dom = lax.axis_index("dom")
    grp = lax.axis_index("grp")
    at_y = dom // width_x
    at_x = lax.rem(dom, width_x)
    upper = lax.rem(grp + 1, groups)
    lower = lax.rem(grp + groups - 1, groups)

    ins = [
        pltpu.make_async_copy(source, target, in_sem.at[at])
        for at, (source, target) in enumerate(
            [
                (send_hbm, send),
                (halo_hbm, halo),
                (features_hbm, features),
                (neighbours_hbm, neighbours),
                (degree_hbm, degree),
                (w_self_hbm, w_self),
                (w_neigh_hbm, w_neigh),
                (bias_hbm, bias),
                (cotangent_hbm, cotangent),
            ]
        )
    ]
    for copy in ins:
        copy.start()

    barrier = pltpu.get_barrier_semaphore()

    def greet_dom(step, carry):
        peer = lax.rem(dom + step, partitions)
        pl.semaphore_signal(barrier, inc=1, device_id=(peer, grp), device_id_type=MESH)
        return carry

    def greet_grp(step, carry):
        peer = lax.rem(grp + step, groups)
        pl.semaphore_signal(barrier, inc=1, device_id=(dom, peer), device_id_type=MESH)
        return carry

    lax.fori_loop(1, partitions, greet_dom, 0)
    lax.fori_loop(1, groups, greet_grp, 0)

    ins[0].wait()
    ins[1].wait()
    per_tile = feat // send_count
    tiled = jnp.concatenate([send[...]] * per_tile, axis=1)
    lane = lax.broadcasted_iota(jnp.int32, (per_tile, feat), 1)
    row = lax.broadcasted_iota(jnp.int32, (per_tile, feat), 0)
    own = row == lane // send_count
    index_rows = [halo[...]]
    for tile in range(partitions // per_tile):
        block = tiled[tile * per_tile : (tile + 1) * per_tile]
        index_rows.append(jnp.sum(jnp.where(own, block, 0), axis=0, keepdims=True))
    node_row = lax.broadcasted_iota(jnp.int32, (node_count, feat), 0)
    node_lane = lax.broadcasted_iota(jnp.int32, (feat, node_count), 1)
    ins[2].wait()
    feature_pair = beside(features[...])
    for at, index_row in enumerate(index_rows):
        listed = pl.ds(at * feat, feat)
        index_column = jnp.broadcast_to(index_row, (feat, feat)).T[:, :1]
        pick = jnp.where(index_column == node_lane, 1.0, 0.0).astype(BF16)
        outgoing[listed, :] = folded_columns(matmul(pick, feature_pair))
        placement[:, listed] = jnp.where(index_row == node_row, 1.0, 0.0).astype(BF16)

    pl.semaphore_wait(barrier, partitions + groups - 2)

    def to_dom(source, target, sem, peer):
        return pltpu.make_async_remote_copy(
            src_ref=source,
            dst_ref=target,
            send_sem=send_sem.at[sem],
            recv_sem=recv_sem.at[sem],
            device_id=(peer, grp),
            device_id_type=MESH,
        )

    def to_grp(source, target, sem, peer):
        return pltpu.make_async_remote_copy(
            src_ref=source,
            dst_ref=target,
            send_sem=send_sem.at[sem],
            recv_sem=recv_sem.at[sem],
            device_id=(dom, peer),
            device_id_type=MESH,
        )

    def peer_dom(step):
        peer_y = lax.rem(at_y + step // width_x, width_y)
        peer_x = lax.rem(at_x + lax.rem(step, width_x), width_x)
        return peer_y * width_x + peer_x

    def send_forward(step, carry):
        peer = peer_dom(step)
        to_dom(
            outgoing.at[pl.ds(halo_count + peer * send_count, send_count)],
            table.at[pl.ds(2 * halo_count + dom * send_count, send_count)],
            0,
            peer,
        ).start()
        return carry

    shared = outgoing.at[pl.ds(0, halo_count)]
    halo_up = to_grp(shared, table.at[pl.ds(0, halo_count)], 1, upper)
    halo_down = to_grp(shared, table.at[pl.ds(halo_count, halo_count)], 2, lower)
    lax.fori_loop(1, partitions, send_forward, 0)
    halo_up.start()
    halo_down.start()
    table[pl.ds(2 * halo_count + dom * send_count, send_count), :] = outgoing[
        pl.ds(halo_count + dom * send_count, send_count), :
    ]

    ins[3].wait()
    ins[4].wait()
    slot = lax.broadcasted_iota(jnp.int32, (slot_count, node_count), 0)
    live = jnp.where(slot < degree[...], neighbours[...], -1)
    inverse_degree = 1.0 / degree[...].astype(F32)
    block_rows = 16

    def count_block(step, carry):
        base = pl.multiple_of(step * block_rows, block_rows)
        rows = base + lax.broadcasted_iota(jnp.int32, (block_rows, node_count), 0)
        total = jnp.zeros((block_rows, node_count), F32)
        for at in range(slot_count):
            total = total + jnp.where(rows == live[at : at + 1], 1.0, 0.0)
        counts[pl.ds(base, block_rows), :] = total.astype(BF16)
        return carry

    lax.fori_loop(0, table_rows // block_rows, count_block, 0)

    features_t = stacked(features[...].T)
    aggregate = folded_rows(matmul(features_t, counts[pl.ds(0, node_count), :]))
    for copy in ins[5:]:
        copy.wait()
    bias_column = jnp.broadcast_to(bias[...], (feat, feat)).T[:, :1]
    pre = folded_rows(matmul(weight_pair(w_self[...].T), features_t)) + bias_column
    neigh_t = weight_pair(w_neigh[...].T)
    neigh = weight_pair(w_neigh[...])
    cotangent_t = cotangent[...].T

    received = to_dom(
        table.at[pl.ds(0, (partitions - 1) * send_count)],
        table.at[pl.ds(0, (partitions - 1) * send_count)],
        0,
        lax.rem(dom + 1, partitions),
    )
    received.wait_recv()
    halo_up.wait_recv()
    halo_down.wait_recv()

    table_t = stacked(table[...].T)
    aggregate = aggregate + folded_rows(
        matmul(table_t, counts[pl.ds(node_count, remote_rows), :])
    )
    aggregate_t = stacked(aggregate * inverse_degree)
    pre = pre + folded_rows(matmul(neigh_t, aggregate_t))

    root = 0.7978845608028654
    square = pre * pre
    bent = jnp.tanh(root * (pre + 0.044715 * (square * pre)))
    rise = 0.5 * (1.0 + bent)
    slope = rise + 0.5 * pre * (1.0 - bent * bent) * (root * (1.0 + 3.0 * 0.044715 * square))
    pre_grad = stacked(cotangent_t * slope)

    edge_grad = stacked(folded_rows(matmul(neigh, pre_grad)) * inverse_degree)
    table_grad[...] = folded_columns(
        matmul_nt(counts[pl.ds(node_count, remote_rows), :], edge_grad)
    )

    def send_backward(step, carry):
        peer = peer_dom(step)
        to_dom(
            table_grad.at[pl.ds(2 * halo_count + peer * send_count, send_count)],
            back.at[pl.ds(2 * halo_count + dom * send_count, send_count)],
            3,
            peer,
        ).start()
        return carry

    back_down = to_grp(
        table_grad.at[pl.ds(0, halo_count)], back.at[pl.ds(0, halo_count)], 4, lower
    )
    back_up = to_grp(
        table_grad.at[pl.ds(halo_count, halo_count)],
        back.at[pl.ds(halo_count, halo_count)],
        5,
        upper,
    )
    lax.fori_loop(1, partitions, send_backward, 0)
    back_down.start()
    back_up.start()
    back[pl.ds(2 * halo_count + dom * send_count, send_count), :] = table_grad[
        pl.ds(2 * halo_count + dom * send_count, send_count), :
    ]

    product = folded_columns(
        matmul_nt(jnp.concatenate([features_t, aggregate_t], axis=0), pre_grad)
    )
    weight_grad[pl.ds(0, feat), :] = folded_rows(product[: 2 * feat])
    weight_grad[pl.ds(feat, feat), :] = folded_rows(product[2 * feat :])
    ones = jnp.ones((16, node_count), BF16)
    bias_grad[...] = folded_columns(matmul_nt(ones, pre_grad))[:1]

    def send_scatter(step, carry):
        peer = lax.rem(grp + step, groups)
        to_grp(
            weight_grad.at[pl.ds(peer * piece_rows, piece_rows)],
            scatter_slots.at[pl.ds(grp * piece_rows, piece_rows)],
            6,
            peer,
        ).start()
        to_grp(bias_grad, bias_slots.at[grp], 7, peer).start()
        return carry

    lax.fori_loop(1, groups, send_scatter, 0)
    scatter_slots[pl.ds(grp * piece_rows, piece_rows), :] = weight_grad[
        pl.ds(grp * piece_rows, piece_rows), :
    ]
    bias_slots[grp] = bias_grad[...]

    activated[...] = (pre * rise).T
    out_activated = pltpu.make_async_copy(activated, activated_hbm, out_sem.at[0])
    out_activated.start()
    own_grad = folded_columns(matmul_nt(counts[pl.ds(0, node_count), :], edge_grad))
    own_grad = own_grad + folded_rows(matmul(weight_pair(w_self[...]), pre_grad)).T

    scattered = to_grp(
        scatter_slots.at[pl.ds(0, (groups - 1) * piece_rows)],
        scatter_slots.at[pl.ds(0, (groups - 1) * piece_rows)],
        6,
        upper,
    )
    scattered.wait_recv()
    bias_sent = to_grp(
        bias_slots.at[pl.ds(0, groups - 1)], bias_slots.at[pl.ds(0, groups - 1)], 7, upper
    )
    bias_sent.wait_recv()
    total = scatter_slots[pl.ds(0, piece_rows), :]
    total_bias = bias_slots[0]
    for at in range(1, groups):
        total = total + scatter_slots[pl.ds(at * piece_rows, piece_rows), :]
        total_bias = total_bias + bias_slots[at]
    full_rows = piece_rows + 8

    def put_piece(slots, at, value, value_bias):
        slots[at, pl.ds(0, piece_rows), :] = value
        slots[at, pl.ds(piece_rows, 8), :] = jnp.broadcast_to(value_bias, (8, feat))

    put_piece(x_slots, at_x, total, total_bias)

    def send_x(step, carry):
        peer = at_y * width_x + lax.rem(at_x + step, width_x)
        to_dom(x_slots.at[at_x], x_slots.at[at_x], 8, peer).start()
        return carry

    lax.fori_loop(1, width_x, send_x, 0)
    x_sent = to_dom(
        x_slots.at[pl.ds(0, width_x - 1)],
        x_slots.at[pl.ds(0, width_x - 1)],
        8,
        lax.rem(dom + 1, partitions),
    )
    x_sent.wait_recv()
    total = x_slots[0]
    for at in range(1, width_x):
        total = total + x_slots[at]
    y_slots[at_y] = total

    def send_y(step, carry):
        peer = lax.rem(at_y + step, width_y) * width_x + at_x
        to_dom(y_slots.at[at_y], y_slots.at[at_y], 9, peer).start()
        return carry

    lax.fori_loop(1, width_y, send_y, 0)
    y_sent = to_dom(
        y_slots.at[pl.ds(0, width_y - 1)],
        y_slots.at[pl.ds(0, width_y - 1)],
        9,
        lax.rem(dom + 1, partitions),
    )
    y_sent.wait_recv()
    total = y_slots[0]
    for at in range(1, width_y):
        total = total + y_slots[at]
    total = total * scale
    piece[...] = total[:piece_rows]
    total_b[...] = total[piece_rows : piece_rows + 1]
    out_b = pltpu.make_async_copy(total_b, grad_b_hbm, out_sem.at[1])
    out_b.start()

    def send_gather(step, carry):
        peer = lax.rem(grp + step, groups)
        to_grp(piece, gathered.at[pl.ds(grp * piece_rows, piece_rows)], 10, peer).start()
        return carry

    lax.fori_loop(1, groups, send_gather, 0)
    gathered[pl.ds(grp * piece_rows, piece_rows), :] = piece[...]

    returned = to_dom(
        back.at[pl.ds(0, (partitions - 1) * send_count)],
        back.at[pl.ds(0, (partitions - 1) * send_count)],
        3,
        lax.rem(dom + 1, partitions),
    )
    returned.wait_recv()
    back_down.wait_recv()
    back_up.wait_recv()
    extra = jnp.concatenate(
        [
            back[pl.ds(0, halo_count), :] + back[pl.ds(halo_count, halo_count), :],
            back[pl.ds(2 * halo_count, partitions * send_count), :],
        ],
        axis=0,
    )
    grad_features[...] = own_grad + folded_columns(matmul(placement[...], beside(extra)))
    out_features = pltpu.make_async_copy(grad_features, grad_features_hbm, out_sem.at[2])
    out_features.start()

    collected = to_grp(
        gathered.at[pl.ds(0, (groups - 1) * piece_rows)],
        gathered.at[pl.ds(0, (groups - 1) * piece_rows)],
        10,
        upper,
    )
    collected.wait_recv()
    out_ws = pltpu.make_async_copy(gathered.at[pl.ds(0, feat)], grad_ws_hbm, out_sem.at[3])
    out_wn = pltpu.make_async_copy(gathered.at[pl.ds(feat, feat)], grad_wn_hbm, out_sem.at[4])
    out_ws.start()
    out_wn.start()

    for copy in (
        received,
        halo_up,
        halo_down,
        returned,
        back_down,
        back_up,
        scattered,
        bias_sent,
        x_sent,
        y_sent,
        collected,
    ):
        copy.wait_send()
    for copy in (out_activated, out_b, out_features, out_ws, out_wn):
        copy.wait()


def shards(width_x, features, w_self, w_neigh, bias, cotangent, neighbours, degree, halo_rows, send_rows):
    partitions = lax.axis_size("dom")
    groups = lax.axis_size("grp")
    node_count, feat = features.shape
    hidden = w_self.shape[1]
    halo_count = halo_rows.shape[0]
    send_count = send_rows.shape[3]
    slot_count = neighbours.shape[0]
    remote_rows = 2 * halo_count + partitions * send_count
    listed = halo_count + partitions * send_count
    piece_rows = 2 * feat // groups
    width_y = partitions // width_x
    scale = 1.0 / (node_count * partitions * groups) ** 0.5
    anywhere = pl.BlockSpec(memory_space=pl.ANY)
    activated, grad_features, grad_ws, grad_wn, grad_b = pl.pallas_call(
        functools.partial(kernel, partitions, groups, width_x, scale),
        out_shape=(
            jax.ShapeDtypeStruct((node_count, hidden), F32),
            jax.ShapeDtypeStruct((node_count, feat), F32),
            jax.ShapeDtypeStruct((feat, hidden), F32),
            jax.ShapeDtypeStruct((feat, hidden), F32),
            jax.ShapeDtypeStruct((1, hidden), F32),
        ),
        in_specs=[anywhere] * 9,
        out_specs=(anywhere,) * 5,
        scratch_shapes=[
            pltpu.VMEM((node_count, feat), F32),
            pltpu.VMEM((feat, hidden), F32),
            pltpu.VMEM((feat, hidden), F32),
            pltpu.VMEM((1, hidden), F32),
            pltpu.VMEM((node_count, hidden), F32),
            pltpu.VMEM((slot_count, node_count), jnp.int32),
            pltpu.VMEM((1, node_count), jnp.int32),
            pltpu.VMEM((1, halo_count), jnp.int32),
            pltpu.VMEM((partitions, send_count), jnp.int32),
            pltpu.VMEM((node_count + remote_rows, node_count), BF16),
            pltpu.VMEM((node_count, listed), BF16),
            pltpu.VMEM((listed, feat), F32),
            pltpu.VMEM((remote_rows, feat), F32),
            pltpu.VMEM((remote_rows, feat), F32),
            pltpu.VMEM((remote_rows, feat), F32),
            pltpu.VMEM((node_count, hidden), F32),
            pltpu.VMEM((node_count, feat), F32),
            pltpu.VMEM((2 * feat, hidden), F32),
            pltpu.VMEM((1, hidden), F32),
            pltpu.VMEM((2 * feat, hidden), F32),
            pltpu.VMEM((groups, 1, hidden), F32),
            pltpu.VMEM((width_x, piece_rows + 8, hidden), F32),
            pltpu.VMEM((width_y, piece_rows + 8, hidden), F32),
            pltpu.VMEM((piece_rows, hidden), F32),
            pltpu.VMEM((2 * feat, hidden), F32),
            pltpu.VMEM((1, hidden), F32),
            pltpu.SemaphoreType.DMA((9,)),
            pltpu.SemaphoreType.DMA((5,)),
            pltpu.SemaphoreType.DMA((11,)),
            pltpu.SemaphoreType.DMA((11,)),
        ],
        compiler_params=pltpu.CompilerParams(
            collective_id=0, has_side_effects=True, vmem_limit_bytes=32 * 1024 * 1024
        ),
    )(
        features,
        w_self,
        w_neigh,
        bias.reshape(1, hidden),
        cotangent,
        neighbours,
        degree.reshape(1, node_count),
        halo_rows.reshape(1, halo_count),
        send_rows.reshape(partitions, send_count),
    )
    return activated, grad_features, grad_ws, grad_wn, grad_b.reshape(hidden)


def solution(mesh):
    placed = (
        P(("dom", "grp"), None),
        P(),
        P(),
        P(),
        P(("dom", "grp"), None),
        P(None, ("dom", "grp")),
        P(("dom", "grp")),
        P(("dom", "grp")),
        P("dom", "grp", None, None),
    )
    width_x = 4 if mesh.shape["dom"] % 4 == 0 else 1
    return jax.shard_map(
        functools.partial(shards, width_x),
        mesh=mesh,
        in_specs=placed,
        out_specs=(P(("dom", "grp"), None), P(("dom", "grp"), None), P(), P(), P()),
        check_vma=False,
    )
```

```python
import functools

import jax
import jax.numpy as jnp
from jax import lax
from jax.experimental import pallas as pl
from jax.experimental.pallas import tpu as pltpu
from jax.sharding import PartitionSpec as P

MESH = pl.DeviceIdType.MESH
F32 = jnp.float32
BF16 = jnp.bfloat16
WIDTH_X = 4
WIDTH_C = 2


def halves(value):
    high = value.astype(BF16)
    low = (value - high.astype(F32)).astype(BF16)
    return high, low


def stacked(value):
    return jnp.concatenate(halves(value), axis=0)


def beside(value):
    return jnp.concatenate(halves(value), axis=1)


def folded_rows(product):
    count = product.shape[0] // 2
    return product[:count] + product[count:]


def folded_columns(product):
    count = product.shape[1] // 2
    return product[:, :count] + product[:, count:]


def weight_pair(weight):
    high, low = halves(weight)
    return jnp.concatenate(
        [jnp.concatenate([high, high], axis=1), jnp.concatenate([low, low], axis=1)], axis=0
    )


def matmul(left, right):
    return jnp.dot(left, right, preferred_element_type=F32)


def matmul_nt(left, right):
    return lax.dot_general(left, right, (((1,), (1,)), ((), ())), preferred_element_type=F32)


def far_first(count):
    return sorted(range(count), key=lambda at: (-min(at, count - at), at))


def kernel(
    widths,
    scale,
    features_hbm,
    w_self_hbm,
    w_neigh_hbm,
    bias_hbm,
    cotangent_hbm,
    neighbours_hbm,
    degree_hbm,
    halo_hbm,
    send_hbm,
    activated,
    grad_features,
    gathered,
    total_b,
    features,
    w_self,
    w_neigh,
    bias,
    cotangent,
    neighbours,
    degree,
    halo,
    send,
    counts,
    placement,
    outgoing,
    table,
    table_grad,
    back,
    weight_grad,
    zx_slots,
    x_bias,
    yc_slots,
    yc_bias,
    z_bias,
    piece,
    in_sem,
    send_sem,
    recv_sem,
):
    width_y, width_x, width_z, width_c = widths
    partitions = width_y * width_x
    groups = width_z * width_c
    node_count, feat = features.shape
    halo_count = halo.shape[1]
    send_count = send.shape[0]
    slot_count = neighbours.shape[0]
    remote_rows = table.shape[0]
    table_rows = node_count + remote_rows
    pieces = width_z * width_x
    piece_rows = 2 * feat // pieces
    boundary = 2 * halo_count
    steps = [(step_y, step_x) for step_y in far_first(width_y) for step_x in far_first(width_x)]
    steps.remove((0, 0))
    far_steps = partitions // 2
    far_rows = far_steps * send_count
    near_rows = (partitions - 1 - far_steps) * send_count

    dom = lax.axis_index("dom")
    grp = lax.axis_index("grp")
    at_y = dom // width_x
    at_x = lax.rem(dom, width_x)
    at_z = grp // width_c
    at_c = lax.rem(grp, width_c)
    upper = lax.rem(grp + 1, groups)
    lower = lax.rem(grp + groups - 1, groups)

    def ring(at, count):
        places = [at + over for over in range(count)]
        return [jnp.where(place >= count, place - count, place) for place in places]

    over_y, over_x = ring(at_y, width_y), ring(at_x, width_x)
    over_z, over_c = ring(at_z, width_z), ring(at_c, width_c)

    def dom_at(step):
        return over_y[step[0]] * width_x + over_x[step[1]]

    def dom_before(step):
        return over_y[-step[0]] * width_x + over_x[-step[1]]

    def grp_at(step_z, step_c):
        return over_z[step_z] * width_c + over_c[step_c]

    def apart(step, count):
        return min(step, count - step)

    zx_steps = [(step_z, step_x) for step_z in range(width_z) for step_x in range(width_x)][1:]
    zx_steps.sort(key=lambda step: -apart(step[0], width_z) - apart(step[1], width_x))
    zx_peers = [
        (dom_at((0, step[1])), grp_at(step[0], 0), over_z[step[0]] * width_x + over_x[step[1]])
        for step in zx_steps
    ]
    own_zx = at_z * width_x + at_x
    yc_steps = [(step_y, step_c) for step_y in far_first(width_y) for step_c in range(width_c)]
    yc_steps.remove((0, 0))
    yc_peers = [(dom_at((step[0], 0)), grp_at(0, step[1])) for step in yc_steps]
    own_yc = at_y * width_c + at_c

    ins = [
        pltpu.make_async_copy(source, target, in_sem.at[at])
        for at, (source, target) in enumerate(
            [
                (send_hbm, send),
                (halo_hbm, halo),
                (features_hbm, features),
                (neighbours_hbm, neighbours),
                (degree_hbm, degree),
                (w_self_hbm, w_self),
                (w_neigh_hbm, w_neigh),
                (bias_hbm, bias),
                (cotangent_hbm, cotangent),
            ]
        )
    ]
    for copy in ins:
        copy.start()

    barrier = pltpu.get_barrier_semaphore()
    guests = [(dom_at(step), grp) for step in steps]
    guests += [peer[:2] for step, peer in zip(zx_steps, zx_peers) if step[0] != 0]
    guests += [peer for step, peer in zip(yc_steps, yc_peers) if step[1] != 0]
    guests += [(dom, upper), (dom, lower)]
    for guest in guests:
        pl.semaphore_signal(barrier, inc=1, device_id=guest, device_id_type=MESH)

    ins[0].wait()
    ins[1].wait()
    per_tile = feat // send_count
    tiled = jnp.concatenate([send[...].T] * per_tile, axis=1)
    lane = lax.broadcasted_iota(jnp.int32, (per_tile, feat), 1)
    row = lax.broadcasted_iota(jnp.int32, (per_tile, feat), 0)
    own = row == lane // send_count
    index_rows = [halo[...]]
    for tile in range(partitions // per_tile):
        block = tiled[tile * per_tile : (tile + 1) * per_tile]
        index_rows.append(jnp.sum(jnp.where(own, block, 0), axis=0, keepdims=True))
    node_row = lax.broadcasted_iota(jnp.int32, (node_count, feat), 0)
    node_lane = lax.broadcasted_iota(jnp.int32, (feat, node_count), 1)
    ins[2].wait()
    feature_pair = beside(features[...])
    for at, index_row in enumerate(index_rows):
        listed = pl.ds(at * feat, feat)
        index_column = jnp.broadcast_to(index_row, (feat, feat)).T[:, :1]
        pick = jnp.where(index_column == node_lane, 1.0, 0.0).astype(BF16)
        outgoing[listed, :] = folded_columns(matmul(pick, feature_pair))
        placement[:, listed] = jnp.where(index_row == node_row, 1.0, 0.0).astype(BF16)

    pl.semaphore_wait(barrier, len(guests))

    def copy_to(source, target, sem, peer, group):
        return pltpu.make_async_remote_copy(
            src_ref=source,
            dst_ref=target,
            send_sem=send_sem.at[sem],
            recv_sem=recv_sem.at[sem],
            device_id=(peer, group),
            device_id_type=MESH,
        )

    def all_of(ref, sem):
        return copy_to(ref, ref, sem, dom, upper)

    def send_forward(sem, at):
        peer = dom_at(steps[at])
        copy_to(
            outgoing.at[pl.ds(halo_count + peer * send_count, send_count)],
            table.at[pl.ds(boundary + at * send_count, send_count)],
            sem,
            peer,
            grp,
        ).start()

    shared = outgoing.at[pl.ds(0, halo_count)]
    halo_up = copy_to(shared, table.at[pl.ds(0, halo_count)], 2, dom, upper)
    halo_down = copy_to(shared, table.at[pl.ds(halo_count, halo_count)], 3, dom, lower)
    for at in range(far_steps):
        send_forward(0, at)
    halo_up.start()
    halo_down.start()
    for at in range(far_steps, partitions - 1):
        send_forward(1, at)
    own_rows = pl.ds(boundary + (partitions - 1) * send_count, send_count)
    table[own_rows, :] = outgoing[pl.ds(halo_count + dom * send_count, send_count), :]

    ins[3].wait()
    ins[4].wait()
    slot = lax.broadcasted_iota(jnp.int32, (slot_count, node_count), 0)
    live = jnp.where(slot < degree[...], neighbours[...], -1)
    inverse_degree = 1.0 / degree[...].astype(F32)

    def count_rows(at, first):
        rows = first + lax.broadcasted_iota(jnp.int32, (send_count, node_count), 0)
        total = jnp.zeros((send_count, node_count), F32)
        for at_slot in range(slot_count):
            total = total + jnp.where(rows == live[at_slot : at_slot + 1], 1.0, 0.0)
        counts[pl.ds(at, send_count), :] = total.astype(BF16)

    def count_plain(step, carry):
        at = pl.multiple_of(step * send_count, send_count)
        count_rows(at, at)
        return carry

    lax.fori_loop(0, (node_count + boundary) // send_count, count_plain, 0)
    first = node_count + boundary
    for at, step in enumerate(steps + [(0, 0)]):
        count_rows(first + at * send_count, first + dom_before(step) * send_count)

    features_t = stacked(features[...].T)
    aggregate = folded_rows(matmul(features_t, counts[pl.ds(0, node_count), :]))
    for copy in ins[5:]:
        copy.wait()
    bias_column = jnp.broadcast_to(bias[...], (feat, feat)).T[:, :1]
    pre = folded_rows(matmul(weight_pair(w_self[...].T), features_t)) + bias_column
    neigh_t = weight_pair(w_neigh[...].T)
    neigh = weight_pair(w_neigh[...])
    cotangent_t = cotangent[...].T

    def taken(first, rows):
        return folded_rows(
            matmul(
                stacked(table[pl.ds(first, rows), :].T), counts[pl.ds(node_count + first, rows), :]
            )
        )

    halo_up.wait_recv()
    halo_down.wait_recv()
    sent_near = all_of(table.at[pl.ds(boundary + far_rows, near_rows)], 1)
    sent_near.wait_recv()
    aggregate = aggregate + taken(0, boundary)
    aggregate = aggregate + taken(boundary + far_rows, near_rows + send_count)
    sent_far = all_of(table.at[pl.ds(boundary, far_rows)], 0)
    sent_far.wait_recv()

    aggregate = aggregate + taken(boundary, far_rows)
    aggregate_t = stacked(aggregate * inverse_degree)
    pre = pre + folded_rows(matmul(neigh_t, aggregate_t))

    root = 0.7978845608028654
    square = pre * pre
    bent = jnp.tanh(root * (pre + 0.044715 * (square * pre)))
    rise = 0.5 * (1.0 + bent)
    slope = rise + 0.5 * pre * (1.0 - bent * bent) * (root * (1.0 + 3.0 * 0.044715 * square))
    pre_grad = stacked(cotangent_t * slope)

    product = folded_columns(
        matmul_nt(jnp.concatenate([features_t, aggregate_t], axis=0), pre_grad)
    )
    weight_grad[pl.ds(0, feat), :] = folded_rows(product[: 2 * feat])
    weight_grad[pl.ds(feat, feat), :] = folded_rows(product[2 * feat :])
    for peer, group, number in zx_peers:
        copy_to(
            weight_grad.at[pl.ds(number * piece_rows, piece_rows)],
            zx_slots.at[own_zx],
            7,
            peer,
            group,
        ).start()
    zx_slots[own_zx] = weight_grad[pl.ds(own_zx * piece_rows, piece_rows), :]
    ones = jnp.ones((16, node_count), BF16)
    x_bias[at_x] = folded_columns(matmul_nt(ones, pre_grad))[:1]
    for step in far_first(width_x)[:-1]:
        copy_to(x_bias.at[at_x], x_bias.at[at_x], 8, dom_at((0, step)), grp).start()

    edge_grad = stacked(folded_rows(matmul(neigh, pre_grad)) * inverse_degree)
    table_grad[...] = folded_columns(
        matmul_nt(counts[pl.ds(node_count, remote_rows), :], edge_grad)
    )

    def send_backward(at):
        copy_to(
            table_grad.at[pl.ds(boundary + at * send_count, send_count)],
            back.at[pl.ds(boundary + dom * send_count, send_count)],
            4,
            dom_before(steps[at]),
            grp,
        ).start()

    back_down = copy_to(
        table_grad.at[pl.ds(0, halo_count)], back.at[pl.ds(0, halo_count)], 5, dom, lower
    )
    back_up = copy_to(
        table_grad.at[pl.ds(halo_count, halo_count)],
        back.at[pl.ds(halo_count, halo_count)],
        6,
        dom,
        upper,
    )
    for at in range(partitions - 1):
        send_backward(at)
    back_down.start()
    back_up.start()
    back[pl.ds(boundary + dom * send_count, send_count), :] = table_grad[own_rows, :]

    activated[...] = (pre * rise).T
    own_grad = folded_columns(matmul_nt(counts[pl.ds(0, node_count), :], edge_grad))
    own_grad = own_grad + folded_rows(matmul(weight_pair(w_self[...]), pre_grad)).T

    def summed(slots):
        total = slots[0]
        for at in range(1, slots.shape[0]):
            total = total + slots[at]
        return total

    scattered = all_of(zx_slots.at[pl.ds(0, pieces - 1)], 7)
    scattered.wait_recv()
    yc_slots[own_yc] = summed(zx_slots)
    for peer, group in yc_peers:
        copy_to(yc_slots.at[own_yc], yc_slots.at[own_yc], 9, peer, group).start()
    bias_scattered = all_of(x_bias.at[pl.ds(0, width_x - 1)], 8)
    bias_scattered.wait_recv()
    yc_bias[own_yc] = summed(x_bias)
    for peer, group in yc_peers:
        copy_to(yc_bias.at[own_yc], yc_bias.at[own_yc], 10, peer, group).start()

    yc_sent = all_of(yc_slots.at[pl.ds(0, width_y * width_c - 1)], 9)
    yc_sent.wait_recv()
    own_part = pl.ds(own_zx * piece_rows, piece_rows)
    piece[...] = summed(yc_slots) * scale
    for peer, group, _ in zx_peers:
        copy_to(piece, gathered.at[own_part], 11, peer, group).start()
    gathered[own_part, :] = piece[...]
    yc_bias_sent = all_of(yc_bias.at[pl.ds(0, width_y * width_c - 1)], 10)
    yc_bias_sent.wait_recv()
    z_bias[at_z] = summed(yc_bias)
    for step in far_first(width_z)[:-1]:
        copy_to(z_bias.at[at_z], z_bias.at[at_z], 12, dom, grp_at(step, 0)).start()

    returned = all_of(back.at[pl.ds(0, (partitions - 1) * send_count)], 4)
    returned.wait_recv()
    back_down.wait_recv()
    back_up.wait_recv()
    extra = jnp.concatenate(
        [
            back[pl.ds(0, halo_count), :] + back[pl.ds(halo_count, halo_count), :],
            back[pl.ds(boundary, partitions * send_count), :],
        ],
        axis=0,
    )
    grad_features[...] = own_grad + folded_columns(matmul(placement[...], beside(extra)))
    z_bias_sent = all_of(z_bias.at[pl.ds(0, width_z - 1)], 12)
    z_bias_sent.wait_recv()
    total_b[...] = summed(z_bias) * scale
    collected = all_of(gathered.at[pl.ds(0, (pieces - 1) * piece_rows)], 11)
    collected.wait_recv()

    for copy in (
        sent_far,
        sent_near,
        halo_up,
        halo_down,
        returned,
        back_down,
        back_up,
        scattered,
        bias_scattered,
        yc_sent,
        yc_bias_sent,
        z_bias_sent,
        collected,
    ):
        copy.wait_send()


def put_out(activated, grad_features, gathered, total_b, *rest):
    *outs, out_sem = rest
    feat = gathered.shape[0] // 2
    sources = (
        activated,
        grad_features,
        gathered.at[pl.ds(0, feat)],
        gathered.at[pl.ds(feat, feat)],
        total_b,
    )
    copies = [
        pltpu.make_async_copy(source, target, out_sem.at[at])
        for at, (source, target) in enumerate(zip(sources, outs))
    ]
    for copy in copies:
        copy.start()
    for copy in copies:
        copy.wait()


def shards(features, w_self, w_neigh, bias, cotangent, neighbours, degree, halo_rows, send_rows):
    partitions = lax.axis_size("dom")
    groups = lax.axis_size("grp")
    node_count, feat = features.shape
    hidden = w_self.shape[1]
    halo_count = halo_rows.shape[0]
    send_count = send_rows.shape[3]
    slot_count = neighbours.shape[0]
    remote_rows = 2 * halo_count + partitions * send_count
    listed = halo_count + partitions * send_count
    width_y, width_z = partitions // WIDTH_X, groups // WIDTH_C
    widths = (width_y, WIDTH_X, width_z, WIDTH_C)
    pieces = width_z * WIDTH_X
    piece_rows = 2 * feat // pieces
    scale = 1.0 / (node_count * partitions * groups) ** 0.5
    outside = pl.BlockSpec(memory_space=pltpu.HBM)
    inside = pl.BlockSpec(memory_space=pltpu.VMEM)
    results = pl.pallas_call(
        functools.partial(kernel, widths, scale),
        out_shape=(
            pltpu.VMEM((node_count, hidden), F32),
            pltpu.VMEM((node_count, feat), F32),
            pltpu.VMEM((2 * feat, hidden), F32),
            pltpu.VMEM((1, hidden), F32),
        ),
        in_specs=[outside] * 9,
        out_specs=(inside,) * 4,
        scratch_shapes=[
            pltpu.VMEM((node_count, feat), F32),
            pltpu.VMEM((feat, hidden), F32),
            pltpu.VMEM((feat, hidden), F32),
            pltpu.VMEM((1, hidden), F32),
            pltpu.VMEM((node_count, hidden), F32),
            pltpu.VMEM((slot_count, node_count), jnp.int32),
            pltpu.VMEM((1, node_count), jnp.int32),
            pltpu.VMEM((1, halo_count), jnp.int32),
            pltpu.VMEM((send_count, partitions), jnp.int32),
            pltpu.VMEM((node_count + remote_rows, node_count), BF16),
            pltpu.VMEM((node_count, listed), BF16),
            pltpu.VMEM((listed, feat), F32),
            pltpu.VMEM((remote_rows, feat), F32),
            pltpu.VMEM((remote_rows, feat), F32),
            pltpu.VMEM((remote_rows, feat), F32),
            pltpu.VMEM((2 * feat, hidden), F32),
            pltpu.VMEM((pieces, piece_rows, hidden), F32),
            pltpu.VMEM((WIDTH_X, 1, hidden), F32),
            pltpu.VMEM((width_y * WIDTH_C, piece_rows, hidden), F32),
            pltpu.VMEM((width_y * WIDTH_C, 1, hidden), F32),
            pltpu.VMEM((width_z, 1, hidden), F32),
            pltpu.VMEM((piece_rows, hidden), F32),
            pltpu.SemaphoreType.DMA((9,)),
            pltpu.SemaphoreType.DMA((13,)),
            pltpu.SemaphoreType.DMA((13,)),
        ],
        compiler_params=pltpu.CompilerParams(
            collective_id=0, has_side_effects=True, vmem_limit_bytes=32 * 1024 * 1024
        ),
    )(
        *(
            pltpu.with_memory_space_constraint(value, pltpu.HBM)
            for value in (
                features,
                w_self,
                w_neigh,
                bias.reshape(1, hidden),
                cotangent,
                neighbours,
                degree.reshape(1, node_count),
                halo_rows.reshape(1, halo_count),
                jnp.swapaxes(send_rows, 2, 3).reshape(send_count, partitions),
            )
        )
    )
    activated, grad_features, grad_ws, grad_wn, grad_b = pl.pallas_call(
        put_out,
        out_shape=(
            jax.ShapeDtypeStruct((node_count, hidden), F32),
            jax.ShapeDtypeStruct((node_count, feat), F32),
            jax.ShapeDtypeStruct((feat, hidden), F32),
            jax.ShapeDtypeStruct((feat, hidden), F32),
            jax.ShapeDtypeStruct((1, hidden), F32),
        ),
        in_specs=[inside] * 4,
        out_specs=(outside,) * 5,
        scratch_shapes=[pltpu.SemaphoreType.DMA((5,))],
    )(*(pltpu.with_memory_space_constraint(value, pltpu.VMEM) for value in results))
    return activated, grad_features, grad_ws, grad_wn, grad_b.reshape(hidden)


def solution(mesh):
    placed = (
        P(("dom", "grp"), None),
        P(),
        P(),
        P(),
        P(("dom", "grp"), None),
        P(None, ("dom", "grp")),
        P(("dom", "grp")),
        P(("dom", "grp")),
        P("dom", "grp", None, None),
    )
    return jax.shard_map(
        shards,
        mesh=mesh,
        in_specs=placed,
        out_specs=(P(("dom", "grp"), None), P(("dom", "grp"), None), P(), P(), P()),
        check_vma=False,
    )
```

```python
import functools

import jax
import jax.numpy as jnp
from jax import lax
from jax.experimental import pallas as pl
from jax.experimental.pallas import tpu as pltpu
from jax.sharding import PartitionSpec as P

MESH = pl.DeviceIdType.MESH
F32 = jnp.float32
BF16 = jnp.bfloat16
WIDTH_X = 4
WIDTH_C = 2


def halves(value):
    high = value.astype(BF16)
    low = (value - high.astype(F32)).astype(BF16)
    return high, low


def stacked(value):
    return jnp.concatenate(halves(value), axis=0)


def beside(value):
    return jnp.concatenate(halves(value), axis=1)


def folded_rows(product):
    count = product.shape[0] // 2
    return product[:count] + product[count:]


def folded_columns(product):
    count = product.shape[1] // 2
    return product[:, :count] + product[:, count:]


def weight_pair(weight):
    high, low = halves(weight)
    return jnp.concatenate(
        [jnp.concatenate([high, high], axis=1), jnp.concatenate([low, low], axis=1)], axis=0
    )


def matmul(left, right):
    return jnp.dot(left, right, preferred_element_type=F32)


def matmul_nt(left, right):
    return lax.dot_general(left, right, (((1,), (1,)), ((), ())), preferred_element_type=F32)


def apart(step, count):
    return min(step, count - step)


def far_first(count):
    return sorted(range(count), key=lambda at: -apart(at, count))


def kernel(
    widths,
    scale,
    features_hbm,
    w_self_hbm,
    w_neigh_hbm,
    bias_hbm,
    cotangent_hbm,
    neighbours_hbm,
    degree_hbm,
    halo_hbm,
    send_hbm,
    activated,
    grad_features,
    gathered,
    total_b,
    features,
    w_self,
    w_neigh,
    bias,
    cotangent,
    neighbours,
    degree,
    halo,
    send,
    counts,
    placement,
    outgoing,
    table,
    table_grad,
    back,
    weight_grad,
    sum_slots,
    xc_bias,
    across_slots,
    y_bias,
    z_bias,
    in_sem,
    send_sem,
    recv_sem,
):
    width_y, width_x, width_z, width_c = widths
    partitions = width_y * width_x
    groups = width_z * width_c
    node_count, feat = features.shape
    halo_count = halo.shape[1]
    send_count = send.shape[0]
    slot_count = neighbours.shape[0]
    remote_rows = table.shape[0]
    table_rows = node_count + remote_rows
    pieces = width_z * width_x
    piece_rows = feat // pieces
    boundary = 2 * halo_count
    steps = [(step_y, step_x) for step_y in range(width_y) for step_x in range(width_x)][1:]
    steps.sort(key=lambda step: -apart(step[0], width_y) - apart(step[1], width_x))
    far_steps = partitions // 2
    far_rows = far_steps * send_count
    near_rows = (partitions - 1 - far_steps) * send_count

    dom = lax.axis_index("dom")
    grp = lax.axis_index("grp")
    at_y = dom // width_x
    at_x = lax.rem(dom, width_x)
    at_z = grp // width_c
    at_c = lax.rem(grp, width_c)
    upper = lax.rem(grp + 1, groups)
    lower = lax.rem(grp + groups - 1, groups)

    def ring(at, count):
        places = [at + over for over in range(count)]
        return [jnp.where(place >= count, place - count, place) for place in places]

    over_y, over_x = ring(at_y, width_y), ring(at_x, width_x)
    over_z, over_c = ring(at_z, width_z), ring(at_c, width_c)

    def dom_at(step):
        return over_y[step[0]] * width_x + over_x[step[1]]

    def dom_before(step):
        return over_y[-step[0]] * width_x + over_x[-step[1]]

    def grp_at(step_z, step_c):
        return over_z[step_z] * width_c + over_c[step_c]

    first_core = at_c == 0
    along, across = jnp.where(first_core, at_z, at_y), jnp.where(first_core, at_y, at_z)
    own_number = along * width_x + at_x
    own_piece = jnp.where(first_core, 0, pieces) + own_number
    own_source = own_number * width_c + at_c
    x_steps = [(step, step_x) for step in range(width_z) for step_x in range(width_x)][1:]
    x_steps.sort(key=lambda step: -apart(step[0], width_z) - apart(step[1], width_x))
    xc_peers = [
        (dom_at((0, step_x)), grp_at(0, step_c))
        for step_x in far_first(width_x)
        for step_c in range(width_c)
        if (step_x, step_c) != (0, 0)
    ]
    y_peers = [(dom_at((step, 0)), grp) for step in far_first(width_y)[:-1]]
    z_peers = [(dom, grp_at(step, 0)) for step in far_first(width_z)[:-1]]

    ins = [
        pltpu.make_async_copy(source, target, in_sem.at[at])
        for at, (source, target) in enumerate(
            [
                (send_hbm, send),
                (halo_hbm, halo),
                (features_hbm, features),
                (neighbours_hbm, neighbours),
                (degree_hbm, degree),
                (w_self_hbm, w_self),
                (w_neigh_hbm, w_neigh),
                (bias_hbm, bias),
                (cotangent_hbm, cotangent),
            ]
        )
    ]
    for copy in ins:
        copy.start()

    barrier = pltpu.get_barrier_semaphore()
    offsets = [(step_y, step_x, 0, 0) for step_y, step_x in steps]
    offsets += [(0, step_x, step, step_c) for step, step_x in x_steps for step_c in range(width_c) if step]
    offsets += [(step_y, step_x, 0, 1) for step_y, step_x in steps + [(0, 0)]]
    offsets.sort(key=lambda at: sum(map(apart, at, (width_y, width_x, width_z, width_c))), reverse=True)
    guests = [(dom_at(at[:2]), grp_at(*at[2:])) for at in offsets]
    for guest in guests:
        pl.semaphore_signal(barrier, inc=1, device_id=guest, device_id_type=MESH)

    ins[0].wait()
    ins[1].wait()
    per_tile = feat // send_count
    tiled = jnp.concatenate([send[...].T] * per_tile, axis=1)
    lane = lax.broadcasted_iota(jnp.int32, (per_tile, feat), 1)
    row = lax.broadcasted_iota(jnp.int32, (per_tile, feat), 0)
    own = row == lane // send_count
    index_rows = [halo[...]]
    for tile in range(partitions // per_tile):
        block = tiled[tile * per_tile : (tile + 1) * per_tile]
        index_rows.append(jnp.sum(jnp.where(own, block, 0), axis=0, keepdims=True))
    node_row = lax.broadcasted_iota(jnp.int32, (node_count, feat), 0)
    node_lane = lax.broadcasted_iota(jnp.int32, (feat, node_count), 1)
    ins[2].wait()
    feature_pair = beside(features[...])
    for at, index_row in enumerate(index_rows):
        listed = pl.ds(at * feat, feat)
        index_column = jnp.broadcast_to(index_row, (feat, feat)).T[:, :1]
        pick = jnp.where(index_column == node_lane, 1.0, 0.0).astype(BF16)
        outgoing[listed, :] = folded_columns(matmul(pick, feature_pair))
        placement[:, listed] = jnp.where(index_row == node_row, 1.0, 0.0).astype(BF16)

    pl.semaphore_wait(barrier, len(guests))

    def copy_to(source, target, sem, peer, group):
        return pltpu.make_async_remote_copy(
            src_ref=source,
            dst_ref=target,
            send_sem=send_sem.at[sem],
            recv_sem=recv_sem.at[sem],
            device_id=(peer, group),
            device_id_type=MESH,
        )

    def all_of(ref, sem):
        return copy_to(ref, ref, sem, dom, upper)

    def send_forward(sem, at):
        peer = dom_at(steps[at])
        copy_to(
            outgoing.at[pl.ds(halo_count + peer * send_count, send_count)],
            table.at[pl.ds(boundary + at * send_count, send_count)],
            sem,
            peer,
            grp,
        ).start()

    shared = outgoing.at[pl.ds(0, halo_count)]
    halo_up = copy_to(shared, table.at[pl.ds(0, halo_count)], 2, dom, upper)
    halo_down = copy_to(shared, table.at[pl.ds(halo_count, halo_count)], 3, dom, lower)
    for at in range(far_steps):
        send_forward(0, at)
    halo_up.start()
    halo_down.start()
    for at in range(far_steps, partitions - 1):
        send_forward(1, at)
    own_rows = pl.ds(boundary + (partitions - 1) * send_count, send_count)
    table[own_rows, :] = outgoing[pl.ds(halo_count + dom * send_count, send_count), :]

    ins[3].wait()
    ins[4].wait()
    slot = lax.broadcasted_iota(jnp.int32, (slot_count, node_count), 0)
    live = jnp.where(slot < degree[...], neighbours[...], -1)
    inverse_degree = 1.0 / degree[...].astype(F32)

    def count_rows(at, first):
        rows = first + lax.broadcasted_iota(jnp.int32, (send_count, node_count), 0)
        total = jnp.zeros((send_count, node_count), F32)
        for at_slot in range(slot_count):
            total = total + jnp.where(rows == live[at_slot : at_slot + 1], 1.0, 0.0)
        counts[pl.ds(at, send_count), :] = total.astype(BF16)

    def count_plain(step, carry):
        at = pl.multiple_of(step * send_count, send_count)
        count_rows(at, at)
        return carry

    lax.fori_loop(0, (node_count + boundary) // send_count, count_plain, 0)
    first = node_count + boundary
    for at, step in enumerate(steps + [(0, 0)]):
        count_rows(first + at * send_count, first + dom_before(step) * send_count)

    features_t = stacked(features[...].T)
    aggregate = folded_rows(matmul(features_t, counts[pl.ds(0, node_count), :]))
    for copy in ins[5:]:
        copy.wait()
    bias_column = jnp.broadcast_to(bias[...], (feat, feat)).T[:, :1]
    pre = folded_rows(matmul(weight_pair(w_self[...].T), features_t)) + bias_column
    neigh_t = weight_pair(w_neigh[...].T)
    neigh = weight_pair(w_neigh[...])
    cotangent_t = cotangent[...].T

    def taken(first, rows):
        return folded_rows(
            matmul(
                stacked(table[pl.ds(first, rows), :].T), counts[pl.ds(node_count + first, rows), :]
            )
        )

    halo_up.wait_recv()
    halo_down.wait_recv()
    aggregate = aggregate + taken(0, boundary)
    sent_far = all_of(table.at[pl.ds(boundary, far_rows)], 0)
    sent_far.wait_recv()
    aggregate = aggregate + taken(boundary, far_rows)
    sent_near = all_of(table.at[pl.ds(boundary + far_rows, near_rows)], 1)
    sent_near.wait_recv()
    aggregate = aggregate + taken(boundary + far_rows, near_rows + send_count)
    aggregate_t = stacked(aggregate * inverse_degree)
    pre = pre + folded_rows(matmul(neigh_t, aggregate_t))

    root = 0.7978845608028654
    square = pre * pre
    bent = jnp.tanh(root * (pre + 0.044715 * (square * pre)))
    rise = 0.5 * (1.0 + bent)
    slope = rise + 0.5 * pre * (1.0 - bent * bent) * (root * (1.0 + 3.0 * 0.044715 * square))
    pre_grad = stacked(cotangent_t * slope)

    product = folded_columns(
        matmul_nt(jnp.concatenate([features_t, aggregate_t], axis=0), pre_grad)
    )
    for half in range(2):
        part = folded_rows(product[2 * feat * half : 2 * feat * (half + 1)])
        for at in range(pieces):
            weight_grad[half * pieces + at] = part[at * piece_rows : (at + 1) * piece_rows]

    def send_piece(number, source, peer, group):
        copy_to(weight_grad.at[number], sum_slots.at[source], 7, peer, group).start()

    for step, step_x in x_steps:
        peer_x = over_x[step_x]
        send_piece(
            over_z[step] * width_x + peer_x,
            (at_z * width_x + at_x) * width_c + at_c,
            at_y * width_x + peer_x,
            over_z[step] * width_c,
        )
        send_piece(
            pieces + over_y[step] * width_x + peer_x,
            (at_y * width_x + at_x) * width_c + at_c,
            over_y[step] * width_x + peer_x,
            at_z * width_c + 1,
        )
    send_piece(
        jnp.where(first_core, pieces, 0) + across * width_x + at_x,
        (across * width_x + at_x) * width_c + at_c,
        dom,
        grp_at(0, 1),
    )
    sum_slots[own_source] = weight_grad[own_piece]
    ones = jnp.ones((16, node_count), BF16)
    own_xc = at_x * width_c + at_c
    xc_bias[own_xc] = folded_columns(matmul_nt(ones, pre_grad))[:1]
    for peer, group in xc_peers:
        copy_to(xc_bias.at[own_xc], xc_bias.at[own_xc], 8, peer, group).start()

    edge_grad = stacked(folded_rows(matmul(neigh, pre_grad)) * inverse_degree)
    table_grad[...] = folded_columns(
        matmul_nt(counts[pl.ds(node_count, remote_rows), :], edge_grad)
    )

    def send_backward(at):
        copy_to(
            table_grad.at[pl.ds(boundary + at * send_count, send_count)],
            back.at[pl.ds(boundary + dom * send_count, send_count)],
            4,
            dom_before(steps[at]),
            grp,
        ).start()

    back_down = copy_to(
        table_grad.at[pl.ds(0, halo_count)], back.at[pl.ds(0, halo_count)], 5, dom, lower
    )
    back_up = copy_to(
        table_grad.at[pl.ds(halo_count, halo_count)],
        back.at[pl.ds(halo_count, halo_count)],
        6,
        dom,
        upper,
    )
    for at in range(partitions - 1):
        send_backward(at)
    back_down.start()
    back_up.start()
    back[pl.ds(boundary + dom * send_count, send_count), :] = table_grad[own_rows, :]

    activated[...] = (pre * rise).T
    own_grad = folded_columns(matmul_nt(counts[pl.ds(0, node_count), :], edge_grad))
    own_grad = own_grad + folded_rows(matmul(weight_pair(w_self[...]), pre_grad)).T

    def in_order(own, at):
        return lambda part: jnp.where(own <= at, part(at + 1), part(at))

    line = []
    for at in range(pieces * width_c - 1):
        pick = in_order(own_source, at)
        peer_a = pick(lambda place: place // (width_x * width_c))
        peer_x = pick(lambda place: place // width_c % width_x)
        peer_c = pick(lambda place: place % width_c)
        peer_y, peer_z = jnp.where(first_core, at_y, peer_a), jnp.where(first_core, peer_a, at_z)
        line.append((peer_y * width_x + peer_x, peer_z * width_c + peer_c))
    across_line = []
    for at in range(width_y - 1):
        place = in_order(across, at)(lambda place: place)
        peer_y, peer_z = jnp.where(first_core, place, at_y), jnp.where(first_core, at_z, place)
        across_line.append((peer_y * width_x + at_x, peer_z * width_c + at_c))

    def summed(slots):
        total = slots[0]
        for at in range(1, slots.shape[0]):
            total = total + slots[at]
        return total

    scattered = all_of(sum_slots.at[pl.ds(0, pieces * width_c - 1)], 7)
    scattered.wait_recv()
    across_slots[across] = summed(sum_slots)
    for peer, group in across_line:
        copy_to(across_slots.at[across], across_slots.at[across], 9, peer, group).start()
    bias_scattered = all_of(xc_bias.at[pl.ds(0, width_x * width_c - 1)], 8)
    bias_scattered.wait_recv()
    y_bias[at_y] = summed(xc_bias)
    for peer, group in y_peers:
        copy_to(y_bias.at[at_y], y_bias.at[at_y], 10, peer, group).start()

    across_sent = all_of(across_slots.at[pl.ds(0, width_y - 1)], 9)
    across_sent.wait_recv()
    gathered[own_piece] = summed(across_slots) * scale
    for peer, group in line:
        copy_to(gathered.at[own_piece], gathered.at[own_piece], 11, peer, group).start()
    y_bias_sent = all_of(y_bias.at[pl.ds(0, width_y - 1)], 10)
    y_bias_sent.wait_recv()
    z_bias[at_z] = summed(y_bias)
    for peer, group in z_peers:
        copy_to(z_bias.at[at_z], z_bias.at[at_z], 12, peer, group).start()

    returned = all_of(back.at[pl.ds(0, (partitions - 1) * send_count)], 4)
    returned.wait_recv()
    back_down.wait_recv()
    back_up.wait_recv()
    extra = jnp.concatenate(
        [
            back[pl.ds(0, halo_count), :] + back[pl.ds(halo_count, halo_count), :],
            back[pl.ds(boundary, partitions * send_count), :],
        ],
        axis=0,
    )
    grad_features[...] = own_grad + folded_columns(matmul(placement[...], beside(extra)))
    z_bias_sent = all_of(z_bias.at[pl.ds(0, width_z - 1)], 12)
    z_bias_sent.wait_recv()
    total_b[...] = summed(z_bias) * scale
    collected = all_of(gathered.at[pl.ds(0, 2 * pieces - 1)], 11)
    collected.wait_recv()

    for copy in (
        sent_far,
        sent_near,
        halo_up,
        halo_down,
        returned,
        back_down,
        back_up,
        scattered,
        bias_scattered,
        across_sent,
        y_bias_sent,
        z_bias_sent,
        collected,
    ):
        copy.wait_send()


def put_out(activated, grad_features, gathered, total_b, *rest):
    *outs, grad_ws, grad_wn, out_sem = rest
    pieces, piece_rows, _ = gathered.shape
    pieces = pieces // 2
    copies = [
        pltpu.make_async_copy(source, target, out_sem.at[at])
        for at, (source, target) in enumerate(
            zip((activated, grad_features, grad_ws, grad_wn, total_b), outs)
        )
    ]
    copies[0].start()
    copies[1].start()
    copies[4].start()
    for half, whole in enumerate((grad_ws, grad_wn)):
        for at in range(pieces):
            whole[pl.ds(at * piece_rows, piece_rows), :] = gathered[half * pieces + at]
        copies[2 + half].start()
    for copy in copies:
        copy.wait()


def shards(features, w_self, w_neigh, bias, cotangent, neighbours, degree, halo_rows, send_rows):
    partitions = lax.axis_size("dom")
    groups = lax.axis_size("grp")
    node_count, feat = features.shape
    hidden = w_self.shape[1]
    halo_count = halo_rows.shape[0]
    send_count = send_rows.shape[3]
    slot_count = neighbours.shape[0]
    remote_rows = 2 * halo_count + partitions * send_count
    listed = halo_count + partitions * send_count
    width_y, width_z = partitions // WIDTH_X, groups // WIDTH_C
    widths = (width_y, WIDTH_X, width_z, WIDTH_C)
    pieces = width_z * WIDTH_X
    piece_rows = feat // pieces
    scale = 1.0 / (node_count * partitions * groups) ** 0.5
    outside = pl.BlockSpec(memory_space=pltpu.HBM)
    inside = pl.BlockSpec(memory_space=pltpu.VMEM)
    results = pl.pallas_call(
        functools.partial(kernel, widths, scale),
        out_shape=(
            pltpu.VMEM((node_count, hidden), F32),
            pltpu.VMEM((node_count, feat), F32),
            pltpu.VMEM((2 * pieces, piece_rows, hidden), F32),
            pltpu.VMEM((1, hidden), F32),
        ),
        in_specs=[outside] * 9,
        out_specs=(inside,) * 4,
        scratch_shapes=[
            pltpu.VMEM((node_count, feat), F32),
            pltpu.VMEM((feat, hidden), F32),
            pltpu.VMEM((feat, hidden), F32),
            pltpu.VMEM((1, hidden), F32),
            pltpu.VMEM((node_count, hidden), F32),
            pltpu.VMEM((slot_count, node_count), jnp.int32),
            pltpu.VMEM((1, node_count), jnp.int32),
            pltpu.VMEM((1, halo_count), jnp.int32),
            pltpu.VMEM((send_count, partitions), jnp.int32),
            pltpu.VMEM((node_count + remote_rows, node_count), BF16),
            pltpu.VMEM((node_count, listed), BF16),
            pltpu.VMEM((listed, feat), F32),
            pltpu.VMEM((remote_rows, feat), F32),
            pltpu.VMEM((remote_rows, feat), F32),
            pltpu.VMEM((remote_rows, feat), F32),
            pltpu.VMEM((2 * pieces, piece_rows, hidden), F32),
            pltpu.VMEM((pieces * WIDTH_C, piece_rows, hidden), F32),
            pltpu.VMEM((WIDTH_X * WIDTH_C, 1, hidden), F32),
            pltpu.VMEM((width_y, piece_rows, hidden), F32),
            pltpu.VMEM((width_y, 1, hidden), F32),
            pltpu.VMEM((width_z, 1, hidden), F32),
            pltpu.SemaphoreType.DMA((9,)),
            pltpu.SemaphoreType.DMA((13,)),
            pltpu.SemaphoreType.DMA((13,)),
        ],
        compiler_params=pltpu.CompilerParams(
            collective_id=0, has_side_effects=True, vmem_limit_bytes=32 * 1024 * 1024
        ),
    )(
        *(
            pltpu.with_memory_space_constraint(value, pltpu.HBM)
            for value in (
                features,
                w_self,
                w_neigh,
                bias.reshape(1, hidden),
                cotangent,
                neighbours,
                degree.reshape(1, node_count),
                halo_rows.reshape(1, halo_count),
                jnp.swapaxes(send_rows, 2, 3).reshape(send_count, partitions),
            )
        )
    )
    activated, grad_features, grad_ws, grad_wn, grad_b = pl.pallas_call(
        put_out,
        out_shape=(
            jax.ShapeDtypeStruct((node_count, hidden), F32),
            jax.ShapeDtypeStruct((node_count, feat), F32),
            jax.ShapeDtypeStruct((feat, hidden), F32),
            jax.ShapeDtypeStruct((feat, hidden), F32),
            jax.ShapeDtypeStruct((1, hidden), F32),
        ),
        in_specs=[inside] * 4,
        out_specs=(outside,) * 5,
        scratch_shapes=[
            pltpu.VMEM((feat, hidden), F32),
            pltpu.VMEM((feat, hidden), F32),
            pltpu.SemaphoreType.DMA((5,)),
        ],
    )(*(pltpu.with_memory_space_constraint(value, pltpu.VMEM) for value in results))
    return activated, grad_features, grad_ws, grad_wn, grad_b.reshape(hidden)


def solution(mesh):
    placed = (
        P(("dom", "grp"), None),
        P(),
        P(),
        P(),
        P(("dom", "grp"), None),
        P(None, ("dom", "grp")),
        P(("dom", "grp")),
        P(("dom", "grp")),
        P("dom", "grp", None, None),
    )
    return jax.shard_map(
        shards,
        mesh=mesh,
        in_specs=placed,
        out_specs=(P(("dom", "grp"), None), P(("dom", "grp"), None), P(), P(), P()),
        check_vma=False,
    )
```

```python
import functools

import jax
import jax.numpy as jnp
from jax import lax
from jax.experimental import pallas as pl
from jax.experimental.pallas import tpu as pltpu
from jax.sharding import PartitionSpec as P

MESH = pl.DeviceIdType.MESH
F32 = jnp.float32
BF16 = jnp.bfloat16
WIDTH_X = 4
WIDTH_C = 2


def halves(value):
    high = value.astype(BF16)
    low = (value - high.astype(F32)).astype(BF16)
    return high, low


def stacked(value):
    return jnp.concatenate(halves(value), axis=0)


def beside(value):
    return jnp.concatenate(halves(value), axis=1)


def folded_rows(product):
    count = product.shape[0] // 2
    return product[:count] + product[count:]


def folded_columns(product):
    count = product.shape[1] // 2
    return product[:, :count] + product[:, count:]


def weight_pair(weight):
    high, low = halves(weight)
    return jnp.concatenate(
        [jnp.concatenate([high, high], axis=1), jnp.concatenate([low, low], axis=1)], axis=0
    )


def matmul(left, right):
    return jnp.dot(left, right, preferred_element_type=F32)


def matmul_nt(left, right):
    return lax.dot_general(left, right, (((1,), (1,)), ((), ())), preferred_element_type=F32)


def apart(step, count):
    return min(step, count - step)


def far_first(count):
    return sorted(range(count), key=lambda at: -apart(at, count))


def kernel(
    widths,
    scale,
    features_hbm,
    w_self_hbm,
    w_neigh_hbm,
    bias_hbm,
    cotangent_hbm,
    neighbours_hbm,
    degree_hbm,
    halo_hbm,
    send_hbm,
    activated,
    grad_features,
    gathered,
    total_b,
    features,
    w_self,
    w_neigh,
    bias,
    cotangent,
    neighbours,
    degree,
    halo,
    send,
    counts,
    placement,
    outgoing,
    table,
    table_grad,
    back,
    weight_grad,
    sum_slots,
    xc_bias,
    across_slots,
    y_bias,
    z_bias,
    in_sem,
    send_sem,
    recv_sem,
):
    width_y, width_x, width_z, width_c = widths
    partitions = width_y * width_x
    groups = width_z * width_c
    node_count, feat = features.shape
    halo_count = halo.shape[1]
    send_count = send.shape[0]
    slot_count = neighbours.shape[0]
    remote_rows = table.shape[0]
    table_rows = node_count + remote_rows
    pieces = width_z * width_x
    piece_rows = feat // pieces
    boundary = 2 * halo_count
    steps = [(step_y, step_x) for step_y in range(width_y) for step_x in range(width_x)][1:]
    steps.sort(key=lambda step: -apart(step[0], width_y) - apart(step[1], width_x))
    far_steps = partitions // 2
    far_rows = far_steps * send_count
    near_rows = (partitions - 1 - far_steps) * send_count

    dom = lax.axis_index("dom")
    grp = lax.axis_index("grp")
    at_y = dom // width_x
    at_x = lax.rem(dom, width_x)
    at_z = grp // width_c
    at_c = lax.rem(grp, width_c)
    upper = lax.rem(grp + 1, groups)
    lower = lax.rem(grp + groups - 1, groups)

    def ring(at, count):
        places = [at + over for over in range(count)]
        return [jnp.where(place >= count, place - count, place) for place in places]

    over_y, over_x = ring(at_y, width_y), ring(at_x, width_x)
    over_z, over_c = ring(at_z, width_z), ring(at_c, width_c)

    def dom_at(step):
        return over_y[step[0]] * width_x + over_x[step[1]]

    def dom_before(step):
        return over_y[-step[0]] * width_x + over_x[-step[1]]

    def grp_at(step_z, step_c):
        return over_z[step_z] * width_c + over_c[step_c]

    first_core = at_c == 0
    along, across = jnp.where(first_core, at_z, at_y), jnp.where(first_core, at_y, at_z)
    own_number = along * width_x + at_x
    own_piece = jnp.where(first_core, 0, pieces) + own_number
    own_source = own_number * width_c + at_c
    x_steps = [(step, step_x) for step in range(width_z) for step_x in range(width_x)][1:]
    x_steps.sort(key=lambda step: -apart(step[0], width_z) - apart(step[1], width_x))
    xc_peers = [
        (dom_at((0, step_x)), grp_at(0, step_c))
        for step_x in far_first(width_x)
        for step_c in range(width_c)
        if (step_x, step_c) != (0, 0)
    ]
    y_peers = [(dom_at((step, 0)), grp) for step in far_first(width_y)[:-1]]
    z_peers = [(dom, grp_at(step, 0)) for step in far_first(width_z)[:-1]]

    ins = [
        pltpu.make_async_copy(source, target, in_sem.at[at])
        for at, (source, target) in enumerate(
            [
                (send_hbm, send),
                (halo_hbm, halo),
                (features_hbm, features),
                (neighbours_hbm, neighbours),
                (degree_hbm, degree),
                (w_self_hbm, w_self),
                (w_neigh_hbm, w_neigh),
                (bias_hbm, bias),
                (cotangent_hbm, cotangent),
            ]
        )
    ]
    for copy in ins:
        copy.start()

    barrier = pltpu.get_barrier_semaphore()
    offsets = [(step_y, step_x, 0, 0) for step_y, step_x in steps]
    offsets += [(0, step_x, step, step_c) for step, step_x in x_steps for step_c in range(width_c) if step]
    offsets += [(step_y, step_x, 0, 1) for step_y, step_x in steps + [(0, 0)]]
    offsets.sort(key=lambda at: sum(map(apart, at, (width_y, width_x, width_z, width_c))), reverse=True)
    guests = [(dom_at(at[:2]), grp_at(*at[2:])) for at in offsets]
    for guest in guests:
        pl.semaphore_signal(barrier, inc=1, device_id=guest, device_id_type=MESH)

    ins[0].wait()
    ins[1].wait()
    per_tile = feat // send_count
    tiled = jnp.concatenate([send[...].T] * per_tile, axis=1)
    lane = lax.broadcasted_iota(jnp.int32, (per_tile, feat), 1)
    row = lax.broadcasted_iota(jnp.int32, (per_tile, feat), 0)
    own = row == lane // send_count
    index_rows = [halo[...]]
    for tile in range(partitions // per_tile):
        block = tiled[tile * per_tile : (tile + 1) * per_tile]
        index_rows.append(jnp.sum(jnp.where(own, block, 0), axis=0, keepdims=True))
    node_row = lax.broadcasted_iota(jnp.int32, (node_count, feat), 0)
    node_lane = lax.broadcasted_iota(jnp.int32, (feat, node_count), 1)
    ins[2].wait()
    feature_pair = beside(features[...])
    for at, index_row in enumerate(index_rows):
        listed = pl.ds(at * feat, feat)
        index_column = jnp.broadcast_to(index_row, (feat, feat)).T[:, :1]
        pick = jnp.where(index_column == node_lane, 1.0, 0.0).astype(BF16)
        outgoing[listed, :] = folded_columns(matmul(pick, feature_pair))
        placement[:, listed] = jnp.where(index_row == node_row, 1.0, 0.0).astype(BF16)

    pl.semaphore_wait(barrier, len(guests))

    def copy_to(source, target, sem, peer, group):
        return pltpu.make_async_remote_copy(
            src_ref=source,
            dst_ref=target,
            send_sem=send_sem.at[sem],
            recv_sem=recv_sem.at[sem],
            device_id=(peer, group),
            device_id_type=MESH,
        )

    def all_of(ref, sem):
        return copy_to(ref, ref, sem, dom, upper)

    def send_forward(sem, at):
        peer = dom_at(steps[at])
        copy_to(
            outgoing.at[pl.ds(halo_count + peer * send_count, send_count)],
            table.at[pl.ds(boundary + at * send_count, send_count)],
            sem,
            peer,
            grp,
        ).start()

    shared = outgoing.at[pl.ds(0, halo_count)]
    halo_up = copy_to(shared, table.at[pl.ds(0, halo_count)], 2, dom, upper)
    halo_down = copy_to(shared, table.at[pl.ds(halo_count, halo_count)], 3, dom, lower)
    for at in range(far_steps):
        send_forward(0, at)
    halo_up.start()
    halo_down.start()
    for at in range(far_steps, partitions - 1):
        send_forward(1, at)
    own_rows = pl.ds(boundary + (partitions - 1) * send_count, send_count)
    table[own_rows, :] = outgoing[pl.ds(halo_count + dom * send_count, send_count), :]

    ins[3].wait()
    ins[4].wait()
    slot = lax.broadcasted_iota(jnp.int32, (slot_count, node_count), 0)
    live = jnp.where(slot < degree[...], neighbours[...], -1)
    inverse_degree = 1.0 / degree[...].astype(F32)

    def count_rows(at, first):
        rows = first + lax.broadcasted_iota(jnp.int32, (send_count, node_count), 0)
        total = jnp.zeros((send_count, node_count), F32)
        for at_slot in range(slot_count):
            total = total + jnp.where(rows == live[at_slot : at_slot + 1], 1.0, 0.0)
        counts[pl.ds(at, send_count), :] = total.astype(BF16)

    def count_plain(step, carry):
        at = pl.multiple_of(step * send_count, send_count)
        count_rows(at, at)
        return carry

    lax.fori_loop(0, (node_count + boundary) // send_count, count_plain, 0)
    first = node_count + boundary
    for at, step in enumerate(steps + [(0, 0)]):
        count_rows(first + at * send_count, first + dom_before(step) * send_count)

    features_t = stacked(features[...].T)
    aggregate = folded_rows(matmul(features_t, counts[pl.ds(0, node_count), :]))
    for copy in ins[5:]:
        copy.wait()
    bias_column = jnp.broadcast_to(bias[...], (feat, feat)).T[:, :1]
    pre = folded_rows(matmul(weight_pair(w_self[...].T), features_t)) + bias_column
    neigh_t = weight_pair(w_neigh[...].T)
    neigh = weight_pair(w_neigh[...])
    cotangent_t = cotangent[...].T

    def taken(first, rows):
        return folded_rows(
            matmul(
                stacked(table[pl.ds(first, rows), :].T), counts[pl.ds(node_count + first, rows), :]
            )
        )

    halo_up.wait_recv()
    halo_down.wait_recv()
    aggregate = aggregate + taken(0, boundary)
    sent_far = all_of(table.at[pl.ds(boundary, far_rows)], 0)
    sent_far.wait_recv()
    aggregate = aggregate + taken(boundary, far_rows)
    sent_near = all_of(table.at[pl.ds(boundary + far_rows, near_rows)], 1)
    sent_near.wait_recv()

    first = boundary + far_rows
    last_rows = near_rows + send_count
    last_t = stacked(table[pl.ds(first, last_rows), :].T)
    root = 0.7978845608028654
    product = 0.0
    pre_grads, active = [], []
    for at in range(0, node_count, node_count // 2):
        some = slice(at, at + node_count // 2)
        last_counts = counts[pl.ds(node_count + first, last_rows), some]
        sum_some = aggregate[:, some] + folded_rows(matmul(last_t, last_counts))
        aggregate_t = stacked(sum_some * inverse_degree[:, some])
        pre_some = pre[:, some] + folded_rows(matmul(neigh_t, aggregate_t))
        square = pre_some * pre_some
        bent = jnp.tanh(root * (pre_some + 0.044715 * (square * pre_some)))
        rise = 0.5 * (1.0 + bent)
        slope = rise + 0.5 * pre_some * (1.0 - bent * bent) * (
            root * (1.0 + 3.0 * 0.044715 * square)
        )
        pre_grads.append(stacked(cotangent_t[:, some] * slope))
        active.append(pre_some * rise)
        both = jnp.concatenate([features_t[:, some], aggregate_t], axis=0)
        product = product + matmul_nt(both, pre_grads[-1])
    pre_grad = jnp.concatenate(pre_grads, axis=1)

    product = folded_columns(product)
    for half in range(2):
        part = folded_rows(product[2 * feat * half : 2 * feat * (half + 1)])
        for at in range(pieces):
            weight_grad[half * pieces + at] = part[at * piece_rows : (at + 1) * piece_rows]

    def send_piece(number, source, peer, group):
        copy_to(weight_grad.at[number], sum_slots.at[source], 7, peer, group).start()

    for step, step_x in x_steps:
        peer_x = over_x[step_x]
        send_piece(
            over_z[step] * width_x + peer_x,
            (at_z * width_x + at_x) * width_c + at_c,
            at_y * width_x + peer_x,
            over_z[step] * width_c,
        )
        send_piece(
            pieces + over_y[step] * width_x + peer_x,
            (at_y * width_x + at_x) * width_c + at_c,
            over_y[step] * width_x + peer_x,
            at_z * width_c + 1,
        )
    send_piece(
        jnp.where(first_core, pieces, 0) + across * width_x + at_x,
        (across * width_x + at_x) * width_c + at_c,
        dom,
        grp_at(0, 1),
    )
    sum_slots[own_source] = weight_grad[own_piece]
    ones = jnp.ones((16, node_count), BF16)
    own_xc = at_x * width_c + at_c
    xc_bias[own_xc] = folded_columns(matmul_nt(ones, pre_grad))[:1]
    for peer, group in xc_peers:
        copy_to(xc_bias.at[own_xc], xc_bias.at[own_xc], 8, peer, group).start()

    edge_grad = stacked(folded_rows(matmul(neigh, pre_grad)) * inverse_degree)
    table_grad[...] = folded_columns(
        matmul_nt(counts[pl.ds(node_count, remote_rows), :], edge_grad)
    )

    def send_backward(at):
        copy_to(
            table_grad.at[pl.ds(boundary + at * send_count, send_count)],
            back.at[pl.ds(boundary + dom * send_count, send_count)],
            4,
            dom_before(steps[at]),
            grp,
        ).start()

    back_down = copy_to(
        table_grad.at[pl.ds(0, halo_count)], back.at[pl.ds(0, halo_count)], 5, dom, lower
    )
    back_up = copy_to(
        table_grad.at[pl.ds(halo_count, halo_count)],
        back.at[pl.ds(halo_count, halo_count)],
        6,
        dom,
        upper,
    )
    for at in range(partitions - 1):
        send_backward(at)
    back_down.start()
    back_up.start()
    back[pl.ds(boundary + dom * send_count, send_count), :] = table_grad[own_rows, :]

    activated[...] = jnp.concatenate(active, axis=1).T
    own_grad = folded_columns(matmul_nt(counts[pl.ds(0, node_count), :], edge_grad))
    own_grad = own_grad + folded_rows(matmul(weight_pair(w_self[...]), pre_grad)).T

    def in_order(own, at):
        return lambda part: jnp.where(own <= at, part(at + 1), part(at))

    line = []
    for at in range(pieces * width_c - 1):
        pick = in_order(own_source, at)
        peer_a = pick(lambda place: place // (width_x * width_c))
        peer_x = pick(lambda place: place // width_c % width_x)
        peer_c = pick(lambda place: place % width_c)
        peer_y, peer_z = jnp.where(first_core, at_y, peer_a), jnp.where(first_core, peer_a, at_z)
        line.append((peer_y * width_x + peer_x, peer_z * width_c + peer_c))
    across_line = []
    for at in range(width_y - 1):
        place = in_order(across, at)(lambda place: place)
        peer_y, peer_z = jnp.where(first_core, place, at_y), jnp.where(first_core, at_z, place)
        across_line.append((peer_y * width_x + at_x, peer_z * width_c + at_c))

    def summed(slots):
        total = slots[0]
        for at in range(1, slots.shape[0]):
            total = total + slots[at]
        return total

    scattered = all_of(sum_slots.at[pl.ds(0, pieces * width_c - 1)], 7)
    scattered.wait_recv()
    across_slots[across] = summed(sum_slots)
    for peer, group in across_line:
        copy_to(across_slots.at[across], across_slots.at[across], 9, peer, group).start()
    bias_scattered = all_of(xc_bias.at[pl.ds(0, width_x * width_c - 1)], 8)
    bias_scattered.wait_recv()
    y_bias[at_y] = summed(xc_bias)
    for peer, group in y_peers:
        copy_to(y_bias.at[at_y], y_bias.at[at_y], 10, peer, group).start()

    across_sent = all_of(across_slots.at[pl.ds(0, width_y - 1)], 9)
    across_sent.wait_recv()
    gathered[own_piece] = summed(across_slots) * scale
    for peer, group in line:
        copy_to(gathered.at[own_piece], gathered.at[own_piece], 11, peer, group).start()
    y_bias_sent = all_of(y_bias.at[pl.ds(0, width_y - 1)], 10)
    y_bias_sent.wait_recv()
    z_bias[at_z] = summed(y_bias)
    for peer, group in z_peers:
        copy_to(z_bias.at[at_z], z_bias.at[at_z], 12, peer, group).start()

    returned = all_of(back.at[pl.ds(0, (partitions - 1) * send_count)], 4)
    returned.wait_recv()
    back_down.wait_recv()
    back_up.wait_recv()
    extra = jnp.concatenate(
        [
            back[pl.ds(0, halo_count), :] + back[pl.ds(halo_count, halo_count), :],
            back[pl.ds(boundary, partitions * send_count), :],
        ],
        axis=0,
    )
    grad_features[...] = own_grad + folded_columns(matmul(placement[...], beside(extra)))
    z_bias_sent = all_of(z_bias.at[pl.ds(0, width_z - 1)], 12)
    z_bias_sent.wait_recv()
    total_b[...] = summed(z_bias) * scale
    collected = all_of(gathered.at[pl.ds(0, 2 * pieces - 1)], 11)
    collected.wait_recv()

    for copy in (
        sent_far,
        sent_near,
        halo_up,
        halo_down,
        returned,
        back_down,
        back_up,
        scattered,
        bias_scattered,
        across_sent,
        y_bias_sent,
        z_bias_sent,
        collected,
    ):
        copy.wait_send()


def put_out(activated, grad_features, gathered, total_b, *rest):
    *outs, grad_ws, grad_wn, out_sem = rest
    pieces, piece_rows, _ = gathered.shape
    pieces = pieces // 2
    copies = [
        pltpu.make_async_copy(source, target, out_sem.at[at])
        for at, (source, target) in enumerate(
            zip((activated, grad_features, grad_ws, grad_wn, total_b), outs)
        )
    ]
    copies[0].start()
    copies[1].start()
    copies[4].start()
    for half, whole in enumerate((grad_ws, grad_wn)):
        for at in range(pieces):
            whole[pl.ds(at * piece_rows, piece_rows), :] = gathered[half * pieces + at]
        copies[2 + half].start()
    for copy in copies:
        copy.wait()


def shards(features, w_self, w_neigh, bias, cotangent, neighbours, degree, halo_rows, send_rows):
    partitions = lax.axis_size("dom")
    groups = lax.axis_size("grp")
    node_count, feat = features.shape
    hidden = w_self.shape[1]
    halo_count = halo_rows.shape[0]
    send_count = send_rows.shape[3]
    slot_count = neighbours.shape[0]
    remote_rows = 2 * halo_count + partitions * send_count
    listed = halo_count + partitions * send_count
    width_y, width_z = partitions // WIDTH_X, groups // WIDTH_C
    widths = (width_y, WIDTH_X, width_z, WIDTH_C)
    pieces = width_z * WIDTH_X
    piece_rows = feat // pieces
    scale = 1.0 / (node_count * partitions * groups) ** 0.5
    outside = pl.BlockSpec(memory_space=pltpu.HBM)
    inside = pl.BlockSpec(memory_space=pltpu.VMEM)
    results = pl.pallas_call(
        functools.partial(kernel, widths, scale),
        out_shape=(
            pltpu.VMEM((node_count, hidden), F32),
            pltpu.VMEM((node_count, feat), F32),
            pltpu.VMEM((2 * pieces, piece_rows, hidden), F32),
            pltpu.VMEM((1, hidden), F32),
        ),
        in_specs=[outside] * 9,
        out_specs=(inside,) * 4,
        scratch_shapes=[
            pltpu.VMEM((node_count, feat), F32),
            pltpu.VMEM((feat, hidden), F32),
            pltpu.VMEM((feat, hidden), F32),
            pltpu.VMEM((1, hidden), F32),
            pltpu.VMEM((node_count, hidden), F32),
            pltpu.VMEM((slot_count, node_count), jnp.int32),
            pltpu.VMEM((1, node_count), jnp.int32),
            pltpu.VMEM((1, halo_count), jnp.int32),
            pltpu.VMEM((send_count, partitions), jnp.int32),
            pltpu.VMEM((node_count + remote_rows, node_count), BF16),
            pltpu.VMEM((node_count, listed), BF16),
            pltpu.VMEM((listed, feat), F32),
            pltpu.VMEM((remote_rows, feat), F32),
            pltpu.VMEM((remote_rows, feat), F32),
            pltpu.VMEM((remote_rows, feat), F32),
            pltpu.VMEM((2 * pieces, piece_rows, hidden), F32),
            pltpu.VMEM((pieces * WIDTH_C, piece_rows, hidden), F32),
            pltpu.VMEM((WIDTH_X * WIDTH_C, 1, hidden), F32),
            pltpu.VMEM((width_y, piece_rows, hidden), F32),
            pltpu.VMEM((width_y, 1, hidden), F32),
            pltpu.VMEM((width_z, 1, hidden), F32),
            pltpu.SemaphoreType.DMA((9,)),
            pltpu.SemaphoreType.DMA((13,)),
            pltpu.SemaphoreType.DMA((13,)),
        ],
        compiler_params=pltpu.CompilerParams(
            collective_id=0, has_side_effects=True, vmem_limit_bytes=32 * 1024 * 1024
        ),
    )(
        *(
            pltpu.with_memory_space_constraint(value, pltpu.HBM)
            for value in (
                features,
                w_self,
                w_neigh,
                bias.reshape(1, hidden),
                cotangent,
                neighbours,
                degree.reshape(1, node_count),
                halo_rows.reshape(1, halo_count),
                jnp.swapaxes(send_rows, 2, 3).reshape(send_count, partitions),
            )
        )
    )
    activated, grad_features, grad_ws, grad_wn, grad_b = pl.pallas_call(
        put_out,
        out_shape=(
            jax.ShapeDtypeStruct((node_count, hidden), F32),
            jax.ShapeDtypeStruct((node_count, feat), F32),
            jax.ShapeDtypeStruct((feat, hidden), F32),
            jax.ShapeDtypeStruct((feat, hidden), F32),
            jax.ShapeDtypeStruct((1, hidden), F32),
        ),
        in_specs=[inside] * 4,
        out_specs=(outside,) * 5,
        scratch_shapes=[
            pltpu.VMEM((feat, hidden), F32),
            pltpu.VMEM((feat, hidden), F32),
            pltpu.SemaphoreType.DMA((5,)),
        ],
    )(*(pltpu.with_memory_space_constraint(value, pltpu.VMEM) for value in results))
    return activated, grad_features, grad_ws, grad_wn, grad_b.reshape(hidden)


def solution(mesh):
    placed = (
        P(("dom", "grp"), None),
        P(),
        P(),
        P(),
        P(("dom", "grp"), None),
        P(None, ("dom", "grp")),
        P(("dom", "grp")),
        P(("dom", "grp")),
        P("dom", "grp", None, None),
    )
    return jax.shard_map(
        shards,
        mesh=mesh,
        in_specs=placed,
        out_specs=(P(("dom", "grp"), None), P(("dom", "grp"), None), P(), P(), P()),
        check_vma=False,
    )
```

```python
import functools

import jax
import jax.numpy as jnp
from jax import lax
from jax.experimental import pallas as pl
from jax.experimental.pallas import tpu as pltpu
from jax.sharding import PartitionSpec as P

MESH = pl.DeviceIdType.MESH
F32 = jnp.float32
BF16 = jnp.bfloat16
WIDTH_X = 4
WIDTH_C = 2


def halves(value):
    high = value.astype(BF16)
    low = (value - high.astype(F32)).astype(BF16)
    return high, low


def stacked(value):
    return jnp.concatenate(halves(value), axis=0)


def beside(value):
    return jnp.concatenate(halves(value), axis=1)


def folded_rows(product):
    count = product.shape[0] // 2
    return product[:count] + product[count:]


def folded_columns(product):
    count = product.shape[1] // 2
    return product[:, :count] + product[:, count:]


def weight_pair(weight):
    high, low = halves(weight)
    return jnp.concatenate(
        [jnp.concatenate([high, high], axis=1), jnp.concatenate([low, low], axis=1)], axis=0
    )


def matmul(left, right):
    return jnp.dot(left, right, preferred_element_type=F32)


def matmul_nt(left, right):
    return lax.dot_general(left, right, (((1,), (1,)), ((), ())), preferred_element_type=F32)


def apart(step, count):
    return min(step, count - step)


def far_first(count):
    return sorted(range(count), key=lambda at: -apart(at, count))


def kernel(
    widths,
    scale,
    features_hbm,
    w_self_hbm,
    w_neigh_hbm,
    bias_hbm,
    cotangent_hbm,
    neighbours_hbm,
    degree_hbm,
    halo_hbm,
    send_hbm,
    activated,
    grad_features,
    gathered,
    total_b,
    features,
    w_self,
    w_neigh,
    bias,
    cotangent,
    neighbours,
    degree,
    halo,
    send,
    counts,
    placement,
    outgoing,
    table,
    table_grad,
    back,
    weight_grad,
    sum_slots,
    xc_bias,
    across_slots,
    y_bias,
    z_bias,
    in_sem,
    send_sem,
    recv_sem,
):
    width_y, width_x, width_z, width_c = widths
    partitions = width_y * width_x
    groups = width_z * width_c
    node_count, feat = features.shape
    halo_count = halo.shape[1]
    send_count = send.shape[0]
    slot_count = neighbours.shape[0]
    remote_rows = table.shape[0]
    table_rows = node_count + remote_rows
    pieces = width_z * width_x
    piece_rows = feat // pieces
    boundary = 2 * halo_count
    steps = [(step_y, step_x) for step_y in range(width_y) for step_x in range(width_x)][1:]
    steps.sort(key=lambda step: -apart(step[0], width_y) - apart(step[1], width_x))
    far_steps = partitions // 2
    far_rows = far_steps * send_count
    near_rows = (partitions - 1 - far_steps) * send_count

    dom = lax.axis_index("dom")
    grp = lax.axis_index("grp")
    at_y = dom // width_x
    at_x = lax.rem(dom, width_x)
    at_z = grp // width_c
    at_c = lax.rem(grp, width_c)
    upper = lax.rem(grp + 1, groups)
    lower = lax.rem(grp + groups - 1, groups)

    def ring(at, count):
        places = [at + over for over in range(count)]
        return [jnp.where(place >= count, place - count, place) for place in places]

    over_y, over_x = ring(at_y, width_y), ring(at_x, width_x)
    over_z, over_c = ring(at_z, width_z), ring(at_c, width_c)

    def dom_at(step):
        return over_y[step[0]] * width_x + over_x[step[1]]

    def dom_before(step):
        return over_y[-step[0]] * width_x + over_x[-step[1]]

    def grp_at(step_z, step_c):
        return over_z[step_z] * width_c + over_c[step_c]

    first_core = at_c == 0
    along, across = jnp.where(first_core, at_z, at_y), jnp.where(first_core, at_y, at_z)
    own_number = along * width_x + at_x
    own_piece = jnp.where(first_core, 0, pieces) + own_number
    own_source = own_number * width_c + at_c
    x_steps = [(step, step_x) for step in range(width_z) for step_x in range(width_x)][1:]
    x_steps.sort(key=lambda step: -apart(step[0], width_z) - apart(step[1], width_x))
    xc_peers = [
        (dom_at((0, step_x)), grp_at(0, step_c))
        for step_x in far_first(width_x)
        for step_c in range(width_c)
        if (step_x, step_c) != (0, 0)
    ]
    y_peers = [(dom_at((step, 0)), grp) for step in far_first(width_y)[:-1]]
    z_peers = [(dom, grp_at(step, 0)) for step in far_first(width_z)[:-1]]

    ins = [
        pltpu.make_async_copy(source, target, in_sem.at[at])
        for at, (source, target) in enumerate(
            [
                (send_hbm, send),
                (halo_hbm, halo),
                (features_hbm, features),
                (neighbours_hbm, neighbours),
                (degree_hbm, degree),
                (w_self_hbm, w_self),
                (w_neigh_hbm, w_neigh),
                (bias_hbm, bias),
                (cotangent_hbm, cotangent),
            ]
        )
    ]
    for copy in ins:
        copy.start()

    barrier = pltpu.get_barrier_semaphore()
    offsets = [(step_y, step_x, 0, 0) for step_y, step_x in steps]
    offsets += [(0, step_x, step, step_c) for step, step_x in x_steps for step_c in range(width_c) if step]
    offsets += [(step_y, step_x, 0, 1) for step_y, step_x in steps + [(0, 0)]]
    offsets.sort(key=lambda at: sum(map(apart, at, (width_y, width_x, width_z, width_c))), reverse=True)
    guests = [(dom_at(at[:2]), grp_at(*at[2:])) for at in offsets]
    for guest in guests:
        pl.semaphore_signal(barrier, inc=1, device_id=guest, device_id_type=MESH)

    ins[0].wait()
    ins[1].wait()
    per_tile = feat // send_count
    tiled = jnp.concatenate([send[...].T] * per_tile, axis=1)
    lane = lax.broadcasted_iota(jnp.int32, (per_tile, feat), 1)
    row = lax.broadcasted_iota(jnp.int32, (per_tile, feat), 0)
    own = row == lane // send_count
    index_rows = [halo[...]]
    for tile in range(partitions // per_tile):
        block = tiled[tile * per_tile : (tile + 1) * per_tile]
        index_rows.append(jnp.sum(jnp.where(own, block, 0), axis=0, keepdims=True))
    node_row = lax.broadcasted_iota(jnp.int32, (node_count, feat), 0)
    node_lane = lax.broadcasted_iota(jnp.int32, (feat, node_count), 1)
    ins[2].wait()
    feature_pair = beside(features[...])
    for at, index_row in enumerate(index_rows):
        listed = pl.ds(at * feat, feat)
        index_column = jnp.broadcast_to(index_row, (feat, feat)).T[:, :1]
        pick = jnp.where(index_column == node_lane, 1.0, 0.0).astype(BF16)
        outgoing[listed, :] = folded_columns(matmul(pick, feature_pair))
        placement[:, listed] = jnp.where(index_row == node_row, 1.0, 0.0).astype(BF16)

    pl.semaphore_wait(barrier, len(guests))

    def copy_to(source, target, sem, peer, group):
        return pltpu.make_async_remote_copy(
            src_ref=source,
            dst_ref=target,
            send_sem=send_sem.at[sem],
            recv_sem=recv_sem.at[sem],
            device_id=(peer, group),
            device_id_type=MESH,
        )

    def all_of(ref, sem):
        return copy_to(ref, ref, sem, dom, upper)

    def send_forward(sem, at):
        peer = dom_at(steps[at])
        copy_to(
            outgoing.at[pl.ds(halo_count + peer * send_count, send_count)],
            table.at[pl.ds(boundary + at * send_count, send_count)],
            sem,
            peer,
            grp,
        ).start()

    shared = outgoing.at[pl.ds(0, halo_count)]
    halo_up = copy_to(shared, table.at[pl.ds(0, halo_count)], 2, dom, upper)
    halo_down = copy_to(shared, table.at[pl.ds(halo_count, halo_count)], 3, dom, lower)
    for at in range(far_steps):
        send_forward(0, at)
    halo_up.start()
    halo_down.start()
    for at in range(far_steps, partitions - 1):
        send_forward(1, at)
    own_rows = pl.ds(boundary + (partitions - 1) * send_count, send_count)
    table[own_rows, :] = outgoing[pl.ds(halo_count + dom * send_count, send_count), :]

    ins[3].wait()
    ins[4].wait()
    slot = lax.broadcasted_iota(jnp.int32, (slot_count, node_count), 0)
    live = jnp.where(slot < degree[...], neighbours[...], -1)
    inverse_degree = 1.0 / degree[...].astype(F32)

    def count_rows(at, first):
        rows = first + lax.broadcasted_iota(jnp.int32, (send_count, node_count), 0)
        total = jnp.zeros((send_count, node_count), F32)
        for at_slot in range(slot_count):
            total = total + jnp.where(rows == live[at_slot : at_slot + 1], 1.0, 0.0)
        counts[pl.ds(at, send_count), :] = total.astype(BF16)

    def count_plain(step, carry):
        at = pl.multiple_of(step * send_count, send_count)
        count_rows(at, at)
        return carry

    lax.fori_loop(0, (node_count + boundary) // send_count, count_plain, 0)
    first = node_count + boundary
    for at, step in enumerate(steps + [(0, 0)]):
        count_rows(first + at * send_count, first + dom_before(step) * send_count)

    features_t = stacked(features[...].T)
    aggregate = folded_rows(matmul(features_t, counts[pl.ds(0, node_count), :]))
    for copy in ins[5:]:
        copy.wait()
    bias_column = jnp.broadcast_to(bias[...], (feat, feat)).T[:, :1]
    pre = folded_rows(matmul(weight_pair(w_self[...].T), features_t)) + bias_column
    neigh_t = weight_pair(w_neigh[...].T)
    neigh = weight_pair(w_neigh[...])
    cotangent_t = cotangent[...].T

    def taken(first, rows):
        return folded_rows(
            matmul(
                stacked(table[pl.ds(first, rows), :].T), counts[pl.ds(node_count + first, rows), :]
            )
        )

    halo_up.wait_recv()
    halo_down.wait_recv()
    aggregate = aggregate + taken(0, boundary)
    sent_far = all_of(table.at[pl.ds(boundary, far_rows)], 0)
    sent_far.wait_recv()
    aggregate = aggregate + taken(boundary, far_rows)
    sent_near = all_of(table.at[pl.ds(boundary + far_rows, near_rows)], 1)
    sent_near.wait_recv()

    first = boundary + far_rows
    last_rows = near_rows + send_count
    last_t = stacked(table[pl.ds(first, last_rows), :].T)
    root = 0.7978845608028654
    product = 0.0
    pre_grads, active = [], []
    for at in range(0, node_count, node_count // 2):
        some = slice(at, at + node_count // 2)
        last_counts = counts[pl.ds(node_count + first, last_rows), some]
        sum_some = aggregate[:, some] + folded_rows(matmul(last_t, last_counts))
        aggregate_t = stacked(sum_some * inverse_degree[:, some])
        pre_some = pre[:, some] + folded_rows(matmul(neigh_t, aggregate_t))
        square = pre_some * pre_some
        bent = jnp.tanh(root * (pre_some + 0.044715 * (square * pre_some)))
        rise = 0.5 * (1.0 + bent)
        slope = rise + 0.5 * pre_some * (1.0 - bent * bent) * (
            root * (1.0 + 3.0 * 0.044715 * square)
        )
        pre_grads.append(stacked(cotangent_t[:, some] * slope))
        active.append(pre_some * rise)
        both = jnp.concatenate([features_t[:, some], aggregate_t], axis=0)
        product = product + matmul_nt(both, pre_grads[-1])
    pre_grad = jnp.concatenate(pre_grads, axis=1)

    product = folded_columns(product)
    for half in range(2):
        part = folded_rows(product[2 * feat * half : 2 * feat * (half + 1)])
        for at in range(pieces):
            weight_grad[half * pieces + at] = part[at * piece_rows : (at + 1) * piece_rows]

    def send_piece(number, source, peer, group):
        copy_to(weight_grad.at[number], sum_slots.at[source], 7, peer, group).start()

    for step, step_x in x_steps:
        peer_x = over_x[step_x]
        send_piece(
            over_z[step] * width_x + peer_x,
            (at_z * width_x + at_x) * width_c + at_c,
            at_y * width_x + peer_x,
            over_z[step] * width_c,
        )
        send_piece(
            pieces + over_y[step] * width_x + peer_x,
            (at_y * width_x + at_x) * width_c + at_c,
            over_y[step] * width_x + peer_x,
            at_z * width_c + 1,
        )
    send_piece(
        jnp.where(first_core, pieces, 0) + across * width_x + at_x,
        (across * width_x + at_x) * width_c + at_c,
        dom,
        grp_at(0, 1),
    )
    sum_slots[own_source] = weight_grad[own_piece]
    ones = jnp.ones((16, node_count), BF16)
    own_xc = at_x * width_c + at_c
    xc_bias[own_xc] = folded_columns(matmul_nt(ones, pre_grad))[:1]
    for peer, group in xc_peers:
        copy_to(xc_bias.at[own_xc], xc_bias.at[own_xc], 8, peer, group).start()

    edge_grad = stacked(folded_rows(matmul(neigh, pre_grad)) * inverse_degree)

    def put_rows(first, rows):
        table_grad[pl.ds(first, rows), :] = folded_columns(
            matmul_nt(counts[pl.ds(node_count + first, rows), :], edge_grad)
        )

    def send_backward(at):
        copy_to(
            table_grad.at[pl.ds(boundary + at * send_count, send_count)],
            back.at[pl.ds(boundary + dom * send_count, send_count)],
            4,
            dom_before(steps[at]),
            grp,
        ).start()

    back_down = copy_to(
        table_grad.at[pl.ds(0, halo_count)], back.at[pl.ds(0, halo_count)], 5, dom, lower
    )
    back_up = copy_to(
        table_grad.at[pl.ds(halo_count, halo_count)],
        back.at[pl.ds(halo_count, halo_count)],
        6,
        dom,
        upper,
    )
    put_rows(boundary, far_rows)
    for at in range(far_steps):
        send_backward(at)
    put_rows(boundary + far_rows, near_rows + send_count)
    for at in range(far_steps, partitions - 1):
        send_backward(at)
    back[pl.ds(boundary + dom * send_count, send_count), :] = table_grad[own_rows, :]

    activated[...] = jnp.concatenate(active, axis=1).T
    own_grad = folded_columns(matmul_nt(counts[pl.ds(0, node_count), :], edge_grad))
    own_grad = own_grad + folded_rows(matmul(weight_pair(w_self[...]), pre_grad)).T

    def in_order(own, at):
        return lambda part: jnp.where(own <= at, part(at + 1), part(at))

    line = []
    for at in range(pieces * width_c - 1):
        pick = in_order(own_source, at)
        peer_a = pick(lambda place: place // (width_x * width_c))
        peer_x = pick(lambda place: place // width_c % width_x)
        peer_c = pick(lambda place: place % width_c)
        peer_y, peer_z = jnp.where(first_core, at_y, peer_a), jnp.where(first_core, peer_a, at_z)
        line.append((peer_y * width_x + peer_x, peer_z * width_c + peer_c))
    across_line = []
    for at in range(width_y - 1):
        place = in_order(across, at)(lambda place: place)
        peer_y, peer_z = jnp.where(first_core, place, at_y), jnp.where(first_core, at_z, place)
        across_line.append((peer_y * width_x + at_x, peer_z * width_c + at_c))

    def summed(slots):
        total = slots[0]
        for at in range(1, slots.shape[0]):
            total = total + slots[at]
        return total

    scattered = all_of(sum_slots.at[pl.ds(0, pieces * width_c - 1)], 7)
    scattered.wait_recv()
    across_slots[across] = summed(sum_slots)
    for peer, group in across_line:
        copy_to(across_slots.at[across], across_slots.at[across], 9, peer, group).start()
    put_rows(0, boundary)
    back_down.start()
    back_up.start()
    bias_scattered = all_of(xc_bias.at[pl.ds(0, width_x * width_c - 1)], 8)
    bias_scattered.wait_recv()
    y_bias[at_y] = summed(xc_bias)
    for peer, group in y_peers:
        copy_to(y_bias.at[at_y], y_bias.at[at_y], 10, peer, group).start()

    across_sent = all_of(across_slots.at[pl.ds(0, width_y - 1)], 9)
    across_sent.wait_recv()
    gathered[own_piece] = summed(across_slots) * scale
    for peer, group in line:
        copy_to(gathered.at[own_piece], gathered.at[own_piece], 11, peer, group).start()
    y_bias_sent = all_of(y_bias.at[pl.ds(0, width_y - 1)], 10)
    y_bias_sent.wait_recv()
    z_bias[at_z] = summed(y_bias)
    for peer, group in z_peers:
        copy_to(z_bias.at[at_z], z_bias.at[at_z], 12, peer, group).start()

    returned = all_of(back.at[pl.ds(0, (partitions - 1) * send_count)], 4)
    returned.wait_recv()
    back_down.wait_recv()
    back_up.wait_recv()
    extra = jnp.concatenate(
        [
            back[pl.ds(0, halo_count), :] + back[pl.ds(halo_count, halo_count), :],
            back[pl.ds(boundary, partitions * send_count), :],
        ],
        axis=0,
    )
    grad_features[...] = own_grad + folded_columns(matmul(placement[...], beside(extra)))
    z_bias_sent = all_of(z_bias.at[pl.ds(0, width_z - 1)], 12)
    z_bias_sent.wait_recv()
    total_b[...] = summed(z_bias) * scale
    collected = all_of(gathered.at[pl.ds(0, 2 * pieces - 1)], 11)
    collected.wait_recv()

    for copy in (
        sent_far,
        sent_near,
        halo_up,
        halo_down,
        returned,
        back_down,
        back_up,
        scattered,
        bias_scattered,
        across_sent,
        y_bias_sent,
        z_bias_sent,
        collected,
    ):
        copy.wait_send()


def put_out(activated, grad_features, gathered, total_b, *rest):
    *outs, grad_ws, grad_wn, out_sem = rest
    pieces, piece_rows, _ = gathered.shape
    pieces = pieces // 2
    copies = [
        pltpu.make_async_copy(source, target, out_sem.at[at])
        for at, (source, target) in enumerate(
            zip((activated, grad_features, grad_ws, grad_wn, total_b), outs)
        )
    ]
    copies[0].start()
    copies[1].start()
    copies[4].start()
    for half, whole in enumerate((grad_ws, grad_wn)):
        for at in range(pieces):
            whole[pl.ds(at * piece_rows, piece_rows), :] = gathered[half * pieces + at]
        copies[2 + half].start()
    for copy in copies:
        copy.wait()


def shards(features, w_self, w_neigh, bias, cotangent, neighbours, degree, halo_rows, send_rows):
    partitions = lax.axis_size("dom")
    groups = lax.axis_size("grp")
    node_count, feat = features.shape
    hidden = w_self.shape[1]
    halo_count = halo_rows.shape[0]
    send_count = send_rows.shape[3]
    slot_count = neighbours.shape[0]
    remote_rows = 2 * halo_count + partitions * send_count
    listed = halo_count + partitions * send_count
    width_y, width_z = partitions // WIDTH_X, groups // WIDTH_C
    widths = (width_y, WIDTH_X, width_z, WIDTH_C)
    pieces = width_z * WIDTH_X
    piece_rows = feat // pieces
    scale = 1.0 / (node_count * partitions * groups) ** 0.5
    outside = pl.BlockSpec(memory_space=pltpu.HBM)
    inside = pl.BlockSpec(memory_space=pltpu.VMEM)
    results = pl.pallas_call(
        functools.partial(kernel, widths, scale),
        out_shape=(
            pltpu.VMEM((node_count, hidden), F32),
            pltpu.VMEM((node_count, feat), F32),
            pltpu.VMEM((2 * pieces, piece_rows, hidden), F32),
            pltpu.VMEM((1, hidden), F32),
        ),
        in_specs=[outside] * 9,
        out_specs=(inside,) * 4,
        scratch_shapes=[
            pltpu.VMEM((node_count, feat), F32),
            pltpu.VMEM((feat, hidden), F32),
            pltpu.VMEM((feat, hidden), F32),
            pltpu.VMEM((1, hidden), F32),
            pltpu.VMEM((node_count, hidden), F32),
            pltpu.VMEM((slot_count, node_count), jnp.int32),
            pltpu.VMEM((1, node_count), jnp.int32),
            pltpu.VMEM((1, halo_count), jnp.int32),
            pltpu.VMEM((send_count, partitions), jnp.int32),
            pltpu.VMEM((node_count + remote_rows, node_count), BF16),
            pltpu.VMEM((node_count, listed), BF16),
            pltpu.VMEM((listed, feat), F32),
            pltpu.VMEM((remote_rows, feat), F32),
            pltpu.VMEM((remote_rows, feat), F32),
            pltpu.VMEM((remote_rows, feat), F32),
            pltpu.VMEM((2 * pieces, piece_rows, hidden), F32),
            pltpu.VMEM((pieces * WIDTH_C, piece_rows, hidden), F32),
            pltpu.VMEM((WIDTH_X * WIDTH_C, 1, hidden), F32),
            pltpu.VMEM((width_y, piece_rows, hidden), F32),
            pltpu.VMEM((width_y, 1, hidden), F32),
            pltpu.VMEM((width_z, 1, hidden), F32),
            pltpu.SemaphoreType.DMA((9,)),
            pltpu.SemaphoreType.DMA((13,)),
            pltpu.SemaphoreType.DMA((13,)),
        ],
        compiler_params=pltpu.CompilerParams(
            collective_id=0, has_side_effects=True, vmem_limit_bytes=32 * 1024 * 1024
        ),
    )(
        *(
            pltpu.with_memory_space_constraint(value, pltpu.HBM)
            for value in (
                features,
                w_self,
                w_neigh,
                bias.reshape(1, hidden),
                cotangent,
                neighbours,
                degree.reshape(1, node_count),
                halo_rows.reshape(1, halo_count),
                jnp.swapaxes(send_rows, 2, 3).reshape(send_count, partitions),
            )
        )
    )
    activated, grad_features, grad_ws, grad_wn, grad_b = pl.pallas_call(
        put_out,
        out_shape=(
            jax.ShapeDtypeStruct((node_count, hidden), F32),
            jax.ShapeDtypeStruct((node_count, feat), F32),
            jax.ShapeDtypeStruct((feat, hidden), F32),
            jax.ShapeDtypeStruct((feat, hidden), F32),
            jax.ShapeDtypeStruct((1, hidden), F32),
        ),
        in_specs=[inside] * 4,
        out_specs=(outside,) * 5,
        scratch_shapes=[
            pltpu.VMEM((feat, hidden), F32),
            pltpu.VMEM((feat, hidden), F32),
            pltpu.SemaphoreType.DMA((5,)),
        ],
    )(*(pltpu.with_memory_space_constraint(value, pltpu.VMEM) for value in results))
    return activated, grad_features, grad_ws, grad_wn, grad_b.reshape(hidden)


def solution(mesh):
    placed = (
        P(("dom", "grp"), None),
        P(),
        P(),
        P(),
        P(("dom", "grp"), None),
        P(None, ("dom", "grp")),
        P(("dom", "grp")),
        P(("dom", "grp")),
        P("dom", "grp", None, None),
    )
    return jax.shard_map(
        shards,
        mesh=mesh,
        in_specs=placed,
        out_specs=(P(("dom", "grp"), None), P(("dom", "grp"), None), P(), P(), P()),
        check_vma=False,
    )
```
